128 devices in a mesh: frames: 4 (over x), tiles: 32 (over y, z, core).
Axes of the slice: x: 4, y: 4, z: 4, core: 2. Of those that a mesh axis runs over, the one named last changes fastest.
Arguments:
- features: bfloat16 [16, 256, 480, 128], P('frames', 'tiles'), may hold values from -6 to 6
- w_conv: bfloat16 [3, 3, 128, 128], replicated, may hold values from -0.1875 to 0.1875
- query_feats: bfloat16 [16384, 128], P(('frames', 'tiles')), may hold values from -6 to 6
- offset_rows: int32 [16, 128], P('frames'), may hold values from 0 to 7
- offset_cols: int32 [16, 128], P('frames'), may hold values from 0 to 471
- owners: int32 [128, 1], replicated, may hold values from 0 to 31; in each aligned block of 128 rows (0 to 127, 128 to 255, ...) at most 12 rows name the same one
- start_frames: int32 [16384], P(('frames', 'tiles')), may hold values from 0 to 15
- w_corr: bfloat16 [81, 384], replicated, may hold values from -0.625 to 0.625
- w_feat: bfloat16 [128, 384], replicated, may hold values from -0.5 to 0.5
- time_embed: float32 [16, 384], replicated, may hold values from -3 to 3
- gain_attn: float32 [384], replicated, may hold values from 0.5 to 1.5
- w_qkv: bfloat16 [384, 1152], replicated, may hold values from -1.0716518 to 1.0716518
- w_attn_out: bfloat16 [384, 384], replicated, may hold values from -0.3125 to 0.3125
- gain_mlp: float32 [384], replicated, may hold values from 0.5 to 1.5
- w_up: bfloat16 [384, 1536], replicated, may hold values from -0.3125 to 0.3125
- w_down: bfloat16 [1536, 384], replicated, may hold values from -0.15625 to 0.15625
Outputs:
- refined: bfloat16 [16384, 16, 384], P(('frames', 'tiles'))
The draws below stay inside these ranges and needn't reach their ends.
Inputs may be any that keep to these rules, and one draw needn't show every extreme that they name: `owners`: no tile owns more than 12 query blocks; some tile owns exactly 12; every tile owns at least one.
All inputs are finite; a program needn't handle non-finite values.
Results may differ from the reference program's by a relative error of at most 0.0066.
Values may be sent and summed in bfloat16 or wider, within the bound.
No kernel may reach another device: no remote copies, remote signals or barrier semaphores. Data moves between devices by JAX's collectives and lax.ppermute only.
A program may use at most 192 MiB of HBM per device.

```python
import math
import jax
import jax.numpy as jnp
import numpy as np
from jax import lax

C = 128
D = 384
HEADS = 8
MLP_UNITS = 1536
WIN = 9
QBLK = 128
WIDTH_COLS = 480
TILE_ROWS = 8
FRAMES = 16
HEIGHT = 256
BLOCKS = 128
TRACKS = 16384
CAP = 12
N_TILES = 32


def draw_w_qkv(key, part):
    base = jnp.clip(jax.random.normal(jax.random.fold_in(key, 11), (D, 3 * D), jnp.float32), -3.5, 3.5) * D ** (-0.5)
    return base.astype(jnp.bfloat16)


def with_ends(values, rng, smallest, top_value):
    shape = values.shape
    spot = [jax.random.randint(jax.random.fold_in(rng, axis), (), 0, shape[axis]) for axis in range(len(shape))]
    values = values.at[tuple(spot)].set(smallest)
    longest = shape.index(max(shape))
    spot[longest] = (spot[longest] + 1) % shape[longest]
    return values.at[tuple(spot)].set(top_value)


def block_scale(key, extent, split, low, high):
    loudness = 1.0
    for axis_at, shards_of in split:
        heights = jax.random.uniform(jax.random.fold_in(jax.random.fold_in(key, 6), axis_at), (shards_of,), jnp.float32, low / len(split), high / len(split))
        loudness = loudness * jnp.repeat(jnp.exp(heights), extent[axis_at] // shards_of).reshape((-1,) + (1,) * (len(extent) - 1 - axis_at))
    return loudness


def routed_block(stream_key, own, number, rows, count, top, limit, lean):
    order = jax.random.permutation(stream_key, count)
    packed, common = shares(count, rows * top, limit, lean, True), shares(count, rows * top, limit, lean, False)
    places = jnp.arange(count)

    def named(sizes, rotation):
        used = int((sizes > 0).sum())
        fixed = max(1, used // 4)
        moved = fixed + (places - fixed + rotation * (used - fixed)) % max(1, count - fixed)
        return jnp.zeros((count,), jnp.int32).at[order[jnp.where(places < fixed, places, moved)]].set(jnp.asarray(sizes, jnp.int32))

    sizes = jnp.where(number % 4 == 0, named(packed, number // 4), named(common, number - number // 4 - 1))
    mixed = jax.random.permutation(jax.random.fold_in(own, 3), count)
    giver, sink = mixed[0:count // 2 * 2:2], mixed[1:count // 2 * 2:2]
    slack = jnp.minimum(sizes[giver] - 1, limit - sizes[sink]) // 2
    slack = jnp.where((giver == order[0]) | (sink == order[0]) | (sizes[sink] == 0), 0, jnp.maximum(slack, 0))
    moved = jax.random.randint(jax.random.fold_in(own, 4), (count // 2,), 0, 1 << 20) % (slack + 1)
    sizes = sizes.at[giver].add(-moved).at[sink].add(moved)
    members = jnp.searchsorted(jnp.cumsum(sizes), jnp.arange(rows * top), side="right").astype(jnp.int32)
    listing = members.reshape(top, rows).T
    listing = listing[jax.random.permutation(jax.random.fold_in(own, 1), rows)]
    rotation = jax.random.randint(jax.random.fold_in(own, 2), (rows, 1), 0, top)
    return jnp.take_along_axis(listing, (jnp.arange(top)[None, :] + rotation) % top, axis=1)


def shares(count, total, limit, slope, full):
    portions = [(1 << 20) // math.isqrt(rank ** slope) + 1 for rank in range(1, count + 1)]
    largest = limit if full else min(limit, max(-(-total // count), total * portions[0] // sum(portions)))
    least = 1 if total - largest >= count - 1 else 0
    given, surplus = [largest] + [least] * (count - 1), total - largest - least * (count - 1)
    while surplus > 0:
        free = [i for i in range(1, count) if given[i] < largest] or [i for i in range(1, count) if given[i] < limit]
        whole, remaining = sum([portions[i] for i in free]), surplus
        for i in free:
            addition = min(limit - given[i], max(1, remaining * portions[i] // whole), surplus)
            given[i] = given[i] + addition
            surplus = surplus - addition
    return np.array(given)


def noise(rng, extent, spread, most, cuts=(), held_as=jnp.bfloat16):
    level = block_scale(rng, extent, cuts, -0.22, 0.18) if cuts else 1.0
    entries = jax.random.normal(rng, extent, jnp.float32) * spread * level
    return jnp.minimum(jnp.maximum(entries, -most), most).astype(held_as)


def setup_inputs(seed: int = 0) -> dict:
    key_of = jax.random.split(jax.random.key(seed), 17)
    features = noise(key_of[0], (FRAMES, HEIGHT, WIDTH_COLS, C), 1.0, 6.0, ((0, 4), (1, 32)))
    w_conv = noise(key_of[1], (3, 3, C, C), (9 * C) ** -0.5, 0.1875)
    query_feats = noise(key_of[2], (TRACKS, C), 1.0, 6.0, ((0, 128),))
    offset_rows = with_ends(jax.random.randint(key_of[3], (FRAMES, BLOCKS), 0, TILE_ROWS), jax.random.fold_in(key_of[3], 1), 0, TILE_ROWS - 1).astype(jnp.int32)
    offset_cols = with_ends(jax.random.randint(key_of[4], (FRAMES, BLOCKS), 0, WIDTH_COLS - WIN + 1), jax.random.fold_in(key_of[4], 1), 0, WIDTH_COLS - WIN).astype(jnp.int32)
    owners_keys = jax.random.split(jax.random.fold_in(key_of[5], 1), BLOCKS // BLOCKS)
    owners_turns = jax.random.permutation(jax.random.fold_in(key_of[5], 3), BLOCKS // BLOCKS)
    owners = jax.vmap(lambda own, number: routed_block(jax.random.fold_in(key_of[5], 2), own, number, BLOCKS, N_TILES, 1, CAP, 2))(owners_keys, owners_turns).reshape((BLOCKS, 1))
    start_frames = with_ends(jax.random.randint(key_of[6], (TRACKS,), 0, FRAMES), jax.random.fold_in(key_of[6], 1), 0, FRAMES - 1).astype(jnp.int32)
    w_corr = noise(key_of[7], (WIN * WIN, D), (WIN * WIN) ** -0.5, 0.625)
    w_feat = noise(key_of[8], (C, D), C ** -0.5, 0.5)
    time_embed = noise(key_of[9], (FRAMES, D), 0.5, 3.0, (), jnp.float32)
    gain_attn = jnp.clip(1.0 + 0.1 * jax.random.normal(key_of[10], (D,), jnp.float32), 0.5, 1.5)
    w_qkv = draw_w_qkv(jax.random.fold_in(key_of[16], 71), 0)
    w_attn_out = noise(key_of[12], (D, D), D ** -0.5, 0.3125)
    gain_mlp = jnp.clip(1.0 + 0.1 * jax.random.normal(key_of[13], (D,), jnp.float32), 0.5, 1.5)
    w_up = noise(key_of[14], (D, MLP_UNITS), D ** -0.5, 0.3125)
    w_down = noise(key_of[15], (MLP_UNITS, D), MLP_UNITS ** -0.5, 0.15625)
    return {"features": features, "w_conv": w_conv, "query_feats": query_feats, "offset_rows": offset_rows, "offset_cols": offset_cols, "owners": owners, "start_frames": start_frames, "w_corr": w_corr, "w_feat": w_feat, "time_embed": time_embed, "gain_attn": gain_attn, "w_qkv": w_qkv, "w_attn_out": w_attn_out, "gain_mlp": gain_mlp, "w_up": w_up, "w_down": w_down}


def conv_frame(frame, w_conv):
    rows, cols, chans = frame.shape
    padded = jnp.pad(frame, ((1, 1), (1, 1), (0, 0)))
    total = jnp.zeros((rows * cols, chans), jnp.float32)
    for a in range(3):
        for b in range(3):
            piece = padded[a:a + rows, b:b + cols].reshape(rows * cols, chans)
            total = total + jnp.dot(piece, w_conv[a, b], preferred_element_type=jnp.float32)
    return total.reshape(rows, cols, chans).astype(jnp.bfloat16)

def rms_scale(values, gain):
    return values * lax.rsqrt(lax.optimization_barrier(jnp.mean(values * values, axis=-1, keepdims=True)) + 1e-06) * gain

def token_layer(tokens, starts, gain_attn, w_qkv, w_attn_out, gain_mlp, w_up, w_down):
    tracks, frames, width = tokens.shape
    head = width // HEADS
    normed = rms_scale(tokens, gain_attn).astype(jnp.bfloat16)
    qkv = jnp.einsum('tfd,de->tfe', normed.astype(jnp.float32), w_qkv.astype(jnp.float32)).astype(jnp.bfloat16)
    query = qkv[..., :width].reshape(tracks, frames, HEADS, head).astype(jnp.float32)
    keys = qkv[..., width:2 * width].reshape(tracks, frames, HEADS, head).astype(jnp.float32)
    values = qkv[..., 2 * width:].reshape(tracks, frames, HEADS, head).astype(jnp.float32)
    scores = jnp.einsum('tfhe,tghe->thfg', query, keys) * head ** (-0.5)
    valid = jnp.arange(frames)[None, :] >= starts[:, None]
    scores = jnp.where(valid[:, None, None, :], scores, -1e+30)
    top = lax.optimization_barrier(jnp.max(scores, axis=-1, keepdims=True))
    weights = jnp.exp(scores - top)
    probs = (weights / lax.optimization_barrier(jnp.sum(weights, axis=-1, keepdims=True))).astype(jnp.bfloat16)
    attended = jnp.einsum('thfg,tghe->tfhe', probs.astype(jnp.float32), values).astype(jnp.bfloat16)
    attended = attended.reshape(tracks, frames, width)
    mixed = tokens + jnp.einsum('tfd,de->tfe', attended.astype(jnp.float32), w_attn_out.astype(jnp.float32))
    normed2 = rms_scale(mixed, gain_mlp).astype(jnp.bfloat16)
    hidden = jax.nn.gelu(jnp.einsum('tfd,de->tfe', normed2.astype(jnp.float32), w_up.astype(jnp.float32)), approximate=True).astype(jnp.bfloat16)
    result = mixed + jnp.einsum('tfe,ed->tfd', hidden.astype(jnp.float32), w_down.astype(jnp.float32))
    return result.astype(jnp.bfloat16)

def reference(features, w_conv, query_feats, offset_rows, offset_cols, owners, start_frames, w_corr, w_feat, time_embed, gain_attn, w_qkv, w_attn_out, gain_mlp, w_up, w_down):
    chans = features.shape[-1]
    conv = lax.map(lambda frame: conv_frame(frame, w_conv), features)
    padded = jnp.pad(conv, ((0, 0), (4, 4), (0, 0), (0, 0)))
    queries = query_feats.reshape(-1, QBLK, chans)

    def frame_patch(frame, row, col):
        zero_start = jnp.zeros((), jnp.int32)
        return lax.dynamic_slice(frame, (row.astype(jnp.int32), col.astype(jnp.int32), zero_start), (WIN, WIN, chans)).reshape(WIN * WIN, chans)

    def block_corr(inputs):
        query, rows, cols, owner = inputs
        base = (owner * TILE_ROWS).astype(jnp.int32)
        patches = jax.vmap(frame_patch)(padded, (base + rows).astype(jnp.int32), cols.astype(jnp.int32))
        corr = jnp.einsum('fkc,qc->fkq', patches.astype(jnp.float32), query.astype(jnp.float32)) * chans ** (-0.5)
        return corr.astype(jnp.bfloat16)
    corr_all = lax.map(block_corr, (queries, offset_rows.T, offset_cols.T, owners[:, 0]))
    starts = start_frames.reshape(-1, QBLK)

    def block_tokens(inputs):
        corr, query, start = inputs
        tokens = jnp.einsum('fkq,kd->qfd', corr.astype(jnp.float32), w_corr.astype(jnp.float32))
        tokens = tokens + jnp.dot(query, w_feat, preferred_element_type=jnp.float32)[:, None, :] + time_embed[None]
        return token_layer(tokens, start, gain_attn, w_qkv, w_attn_out, gain_mlp, w_up, w_down)
    refined = lax.map(block_tokens, (corr_all, queries, starts))
    return refined.reshape(-1, refined.shape[2], refined.shape[3])
```

```python
import functools

import jax
import jax.numpy as jnp
from jax import lax
from jax.experimental import pallas as pl
from jax.experimental.pallas import tpu as pltpu
from jax.sharding import PartitionSpec as P

HEADS = 8
HEAD = 48
WIN = 9
RAW = WIN + 2
CELLS = RAW * RAW
QBLK = 128
CAP = 12
TILE = 8
EDGE = 5
MSG = 56
PIECES = 32
PROWS = 16
SLOT = PIECES * PROWS
CHUNK = 512
F32 = jnp.float32
BF16 = jnp.bfloat16


def window_rows(feat_ref, tmp_ref, dst_ref, base, frame, row0, rows, col):
    wide = feat_ref.shape[2]
    start = pl.multiple_of(jnp.clip((col >> 4) << 4, 0, wide - 32), 16)
    tmp_ref[0:rows, 8:40, :] = feat_ref[frame, row0 : row0 + rows, pl.ds(start, 32), :].astype(F32)
    for i in range(rows):
        dst_ref[base + RAW * i : base + RAW * i + 16, :] = tmp_ref[i, pl.ds(8 + col - start, 16), :]


def edge_kernel(ids_ref, count_ref, cols_ref, feat_ref, up_ref, down_ref, tmp_ref, win_ref):
    frames = feat_ref.shape[0]
    rows = feat_ref.shape[1]
    tmp_ref[...] = jnp.zeros_like(tmp_ref)

    def part(which, row0, out_ref):
        def slot(s, carry):
            block = ids_ref[which, s]
            for k in range(frames):
                window_rows(
                    feat_ref, tmp_ref, win_ref, k * MSG, k, row0, EDGE, cols_ref[k, block] - 1
                )
            out_ref[pl.ds(pl.multiple_of(s * frames * MSG, 16), frames * MSG), :] = win_ref[
                0 : frames * MSG, :
            ].astype(BF16)
            return carry

        lax.fori_loop(0, count_ref[which], slot, 0)

    win_ref[...] = jnp.zeros_like(win_ref)
    part(2, rows - EDGE, up_ref)
    part(0, 0, down_ref)


def merge_kernel(
    ids_ref, count_ref, info_ref, cols_ref, offs_ref, feat_ref, low_ref, high_ref, out_ref,
    tmp_ref, side_ref, win_ref, all_ref,
):
    frames, rows = feat_ref.shape[0], feat_ref.shape[1]
    tmp_ref[...] = jnp.zeros_like(tmp_ref)
    win_ref[...] = jnp.zeros_like(win_ref)

    def slot(s, carry):
        block = ids_ref[1, s]
        here = pl.ds(pl.multiple_of(s * frames * MSG, 16), frames * MSG)
        side_ref[0] = low_ref[here, :].astype(F32)
        side_ref[1] = high_ref[here, :].astype(F32)
        own = EDGE * RAW
        for k in range(frames):
            row = offs_ref[k, block]
            win_ref[0:MSG, :] = side_ref[0, k * MSG : (k + 1) * MSG, :]
            window_rows(feat_ref, tmp_ref, win_ref, own, k, 0, rows, cols_ref[k, block] - 1)
            top = own + rows * RAW
            win_ref[top : top + MSG, :] = side_ref[1, k * MSG : (k + 1) * MSG, :]
            all_ref[k * CELLS : k * CELLS + 128, :] = win_ref[pl.ds(row * RAW, 128), :]
        end = frames * CELLS
        all_ref[end:SLOT, :] = jnp.zeros((SLOT - end, 128), F32)
        for k in range(frames):
            first = (info_ref[0] * rows + offs_ref[k, block] - WIN // 2).astype(F32)
            all_ref[end + k : end + k + 1, :] = jnp.full((1, 128), first, F32)
        for i in range(PIECES):
            out_ref[i, pl.ds(pl.multiple_of(s * PROWS, 16), PROWS), :] = all_ref[
                i * PROWS : (i + 1) * PROWS, :
            ].astype(BF16)
        return carry

    lax.fori_loop(0, count_ref[1], slot, 0)


def route_kernel(owner_ref, rank_ref, in_ref, out_ref):
    def step(b, carry):
        out_ref[b] = in_ref[owner_ref[b], pl.ds(pl.multiple_of(rank_ref[b] * PROWS, 16), PROWS), :]
        return carry

    lax.fori_loop(0, out_ref.shape[0], step, 0, unroll=8)


def nt(a, b):
    return lax.dot_general(a, b, (((1,), (1,)), ((), ())), preferred_element_type=F32)


def rms_scale(values, gain):
    return values * lax.rsqrt(jnp.mean(values * values, axis=-1, keepdims=True) + 1e-06) * gain


def refine_kernel(
    height, raw_ref, wconv_ref, query_ref, wcorr_ref, wfeat_ref, time_ref, start_ref, gain1_ref,
    wk_ref, wq_ref, wv_ref, wout_ref, gain2_ref, wup_ref, wdown_ref, out_ref,
    cells_ref, cols_ref, tok_ref,
):
    groups, per = raw_ref.shape[0] // SLOT, 4
    frames = groups * per
    step = pl.program_id(0)

    @pl.when(step == 0)
    def _():
        cells_ref[0 : groups * SLOT, :] = raw_ref[...].astype(F32)
        cells_ref[groups * SLOT :, :] = jnp.zeros_like(cells_ref[groups * SLOT :, :])
        line = lax.broadcasted_iota(jnp.int32, (128, 128), 0) // RAW
        line = line.astype(F32)
        for f in range(frames):
            base = (f // per) * SLOT + (f % per) * CELLS
            for a in range(3):
                for b in range(3):
                    at = base + a * RAW + b
                    cols_ref[f * 128 : (f + 1) * 128, (a * 3 + b) * 128 : (a * 3 + b + 1) * 128] = (
                        cells_ref[at : at + 128, :].astype(BF16)
                    )
        feat = jnp.dot(query_ref[...], wfeat_ref[...], preferred_element_type=F32)
        for f in range(frames):
            conv = jnp.dot(
                cols_ref[f * 128 : (f + 1) * 128, :], wconv_ref[...], preferred_element_type=F32
            )
            info = (f // per) * SLOT + per * CELLS + f % per
            row = line + cells_ref[info : info + 1, :]
            conv = jnp.where((row >= 0) & (row < height), conv, 0.0).astype(BF16)
            corr = (nt(query_ref[...], conv) * (128 ** -0.5)).astype(BF16)
            tokens = jnp.dot(corr, wcorr_ref[...], preferred_element_type=F32)
            tokens = tokens + feat + time_ref[f : f + 1, :]
            for part in range(3):
                tok_ref[part, pl.ds(f, 128, stride=frames), :] = tokens[
                    :, part * 128 : (part + 1) * 128
                ]

    here = pl.ds(pl.multiple_of(step * CHUNK, CHUNK), CHUNK)
    tokens = jnp.concatenate([tok_ref[part, here, :] for part in range(3)], axis=1)
    normed = rms_scale(tokens, gain1_ref[...]).astype(BF16)
    keys = jnp.dot(normed, wk_ref[...], preferred_element_type=F32).astype(BF16)
    query = nt(wq_ref[...], normed).astype(BF16)
    values = nt(wv_ref[...], normed).astype(BF16)
    track = lax.broadcasted_iota(jnp.int32, (16, 128), 1) // frames
    frame = lax.broadcasted_iota(jnp.int32, (16, 128), 0)
    key_track = lax.broadcasted_iota(jnp.int32, (128, 128), 0) // frames
    query_track = lax.broadcasted_iota(jnp.int32, (128, 128), 1) // frames
    same = (key_track == query_track).astype(BF16)
    factor = HEAD ** -0.5 * 1.4426950408889634
    zeros16 = jnp.zeros((16, 128), BF16)
    zeros64 = jnp.zeros((64, 128), BF16)
    attended = []
    for g in range(CHUNK // 128):
        lanes = slice(g * 128, (g + 1) * 128)
        valid = frame >= start_ref[0, :, lanes]
        heads = []
        for pair in range(HEADS // 2):
            one = query[2 * pair * HEAD : (2 * pair + 1) * HEAD, lanes]
            two = query[(2 * pair + 1) * HEAD : (2 * pair + 2) * HEAD, lanes]
            both = jnp.concatenate(
                [
                    jnp.concatenate([one, zeros16, zeros64], axis=0),
                    jnp.concatenate([zeros64, two, zeros16], axis=0),
                ],
                axis=1,
            )
            scores = jnp.dot(
                keys[lanes, pair * 128 : (pair + 1) * 128], both, preferred_element_type=F32
            )
            for h in range(2):
                full = scores[:, h * 128 : (h + 1) * 128]
                own = full[0:16, :]
                for t in range(1, 8):
                    own = jnp.where(track == t, full[16 * t : 16 * (t + 1), :], own)
                own = jnp.where(valid, own, -1e30)
                top = jnp.max(own, axis=0, keepdims=True)
                weights = jnp.exp2((own - top) * factor)
                probs = (weights / jnp.sum(weights, axis=0, keepdims=True)).astype(BF16)
                spread = jnp.concatenate([probs] * 8, axis=0) * same
                at = (2 * pair + h) * HEAD
                heads.append(
                    jnp.dot(values[at : at + HEAD, lanes], spread, preferred_element_type=F32)
                )
        attended.append(jnp.concatenate(heads, axis=0).T.astype(BF16))
    attended = jnp.concatenate(attended, axis=0)
    mixed = tokens + jnp.dot(attended, wout_ref[...], preferred_element_type=F32)
    normed2 = rms_scale(mixed, gain2_ref[...]).astype(BF16)
    hidden = jax.nn.gelu(
        jnp.dot(normed2, wup_ref[...], preferred_element_type=F32), approximate=True
    ).astype(BF16)
    result = mixed + jnp.dot(hidden, wdown_ref[...], preferred_element_type=F32)
    out_ref[...] = result.astype(BF16)


def params(mib):
    return pltpu.CompilerParams(vmem_limit_bytes=mib << 20)


SMEM = pl.BlockSpec(memory_space=pltpu.SMEM)
VMEM = pl.BlockSpec(memory_space=pltpu.VMEM)


def body(
    features, w_conv, query_feats, offset_rows, offset_cols, owners, start_frames, w_corr, w_feat,
    time_embed, gain_attn, w_qkv, w_attn_out, gain_mlp, w_up, w_down,
):
    n_tiles = lax.axis_size("tiles")
    tile = lax.axis_index("tiles")
    frames, rows, width, chans = features.shape
    blocks = owners.shape[0]
    tracks = query_feats.shape[0]
    total = time_embed.shape[0]
    dim = w_feat.shape[1]

    owner = owners[:, 0]
    number = jnp.arange(blocks, dtype=jnp.int32)
    rank = jnp.sum(
        (owner[:, None] == owner[None, :]) & (number[None, :] < number[:, None]), axis=1, dtype=jnp.int32
    )
    near = tile + jnp.arange(-1, 2, dtype=jnp.int32)
    mine = owner[None, :] == near[:, None]
    count = jnp.sum(mine, axis=1, dtype=jnp.int32)
    slots = jnp.arange(CAP, dtype=jnp.int32)
    ids = jnp.sum(
        jnp.where(mine[:, None, :] & (rank[None, None, :] == slots[None, :, None]), number, 0),
        axis=2,
        dtype=jnp.int32,
    )

    message = jax.ShapeDtypeStruct((CAP * frames * MSG, chans), BF16)
    up, down = pl.pallas_call(
        edge_kernel,
        out_shape=(message, message),
        in_specs=[SMEM, SMEM, SMEM, VMEM],
        out_specs=(VMEM, VMEM),
        scratch_shapes=[pltpu.VMEM((TILE, 48, 128), F32), pltpu.VMEM((frames * MSG + 16, 128), F32)],
        compiler_params=params(24),
        name="edges",
    )(ids, count, offset_cols, features)
    low = lax.ppermute(up, "tiles", [(i, i + 1) for i in range(n_tiles - 1)])
    high = lax.ppermute(down, "tiles", [(i + 1, i) for i in range(n_tiles - 1)])
    pieces = pl.pallas_call(
        merge_kernel,
        out_shape=jax.ShapeDtypeStruct((PIECES, CAP * PROWS, chans), BF16),
        in_specs=[SMEM, SMEM, SMEM, SMEM, SMEM, VMEM, VMEM, VMEM],
        out_specs=VMEM,
        scratch_shapes=[
            pltpu.VMEM((TILE, 48, 128), F32),
            pltpu.VMEM((2, frames * MSG, 128), F32),
            pltpu.VMEM((208, 128), F32),
            pltpu.VMEM((SLOT, 128), F32),
        ],
        compiler_params=params(24),
        name="windows",
    )(ids, count, tile.reshape(1), offset_cols, offset_rows, features, low, high)
    spread = lax.all_to_all(pieces, "tiles", 0, 0, tiled=True)
    routed = pl.pallas_call(
        route_kernel,
        out_shape=jax.ShapeDtypeStruct((blocks, PROWS, chans), BF16),
        in_specs=[SMEM, SMEM, VMEM],
        out_specs=VMEM,
        compiler_params=params(24),
        name="route",
    )(owner, rank, spread)
    raw = lax.all_to_all(routed, ("frames", "tiles"), 0, 0, tiled=True)
    raw = raw.reshape(blocks * PROWS, chans)

    wk = jnp.pad(w_qkv[:, dim : 2 * dim].reshape(dim, HEADS, HEAD), ((0, 0), (0, 0), (0, 16)))
    wk = wk.reshape(dim, HEADS * 64)
    wq, wv = w_qkv[:, :dim].T, w_qkv[:, 2 * dim :].T
    wcorr = jnp.pad(w_corr.reshape(WIN, WIN, dim), ((0, 0), (0, RAW - WIN), (0, 0)))
    wcorr = jnp.pad(wcorr.reshape(WIN * RAW, dim), ((0, 128 - WIN * RAW), (0, 0)))
    tokens = tracks * total
    start = jnp.repeat(start_frames, total).reshape(tokens // CHUNK, 1, CHUNK)
    whole = lambda *shape: pl.BlockSpec(shape, lambda i: (0,) * len(shape))
    refined = pl.pallas_call(
        functools.partial(refine_kernel, n_tiles * rows),
        grid=(tokens // CHUNK,),
        out_shape=jax.ShapeDtypeStruct((tokens, dim), BF16),
        in_specs=[
            whole(blocks * PROWS, chans),
            whole(9 * chans, chans),
            whole(tracks, chans),
            whole(128, dim),
            whole(chans, dim),
            whole(total, dim),
            pl.BlockSpec((1, 1, CHUNK), lambda i: (i, 0, 0)),
            whole(1, dim),
            whole(dim, HEADS * 64),
            whole(dim, dim),
            whole(dim, dim),
            whole(dim, dim),
            whole(1, dim),
            whole(*w_up.shape),
            whole(*w_down.shape),
        ],
        out_specs=pl.BlockSpec((CHUNK, dim), lambda i: (i, 0)),
        scratch_shapes=[
            pltpu.VMEM((blocks * PROWS + 16, 128), F32),
            pltpu.VMEM((total * 128, 9 * chans), BF16),
            pltpu.VMEM((3, tokens, 128), F32),
        ],
        compiler_params=params(56),
        name="refine",
    )(
        raw, w_conv.reshape(9 * chans, chans), query_feats, wcorr, w_feat, time_embed, start,
        gain_attn.reshape(1, dim), wk, wq, wv, w_attn_out, gain_mlp.reshape(1, dim), w_up, w_down,
    )
    return refined.reshape(tracks, total, dim)


def solution(mesh):
    placed = (
        P("frames", "tiles", None, None),
        P(),
        P(("frames", "tiles"), None),
        P("frames", None),
        P("frames", None),
        P(),
        P(("frames", "tiles")),
        P(), P(), P(), P(), P(), P(), P(), P(), P(),
    )
    return jax.shard_map(
        body,
        mesh=mesh,
        in_specs=placed,
        out_specs=P(("frames", "tiles"), None, None),
        check_vma=False,
    )
```

```python
import functools

import jax
import jax.numpy as jnp
from jax import lax
from jax.experimental import pallas as pl
from jax.experimental.pallas import tpu as pltpu
from jax.sharding import PartitionSpec as P

HEADS = 8
HEAD = 48
WIN = 9
RAW = WIN + 2
CELLS = RAW * RAW
QBLK = 128
CAP = 12
TILE = 8
EDGE = 5
MSG = 56
PIECES = 32
PROWS = 16
SLOT = PIECES * PROWS
CHUNK = 1024
BATCH = 4
F32 = jnp.float32
BF16 = jnp.bfloat16


def window_rows(feat_ref, tmp_ref, dst_ref, base, frame, row0, rows, col):
    wide = feat_ref.shape[2]
    start = pl.multiple_of(jnp.clip((col >> 4) << 4, 0, wide - 32), 16)
    tmp_ref[0:rows, 8:40, :] = feat_ref[frame, row0 : row0 + rows, pl.ds(start, 32), :].astype(F32)
    for i in range(rows):
        dst_ref[base + RAW * i : base + RAW * i + 16, :] = tmp_ref[i, pl.ds(8 + col - start, 16), :]


def edge_kernel(ids_ref, count_ref, cols_ref, feat_ref, up_ref, down_ref, tmp_ref, win_ref):
    frames = feat_ref.shape[0]
    rows = feat_ref.shape[1]
    tmp_ref[...] = jnp.zeros_like(tmp_ref)

    def part(which, row0, out_ref):
        def slot(s, carry):
            block = ids_ref[which, s]
            for k in range(frames):
                window_rows(
                    feat_ref, tmp_ref, win_ref, k * MSG, k, row0, EDGE, cols_ref[k, block] - 1
                )
            out_ref[pl.ds(pl.multiple_of(s * frames * MSG, 16), frames * MSG), :] = win_ref[
                0 : frames * MSG, :
            ].astype(BF16)
            return carry

        lax.fori_loop(0, count_ref[which], slot, 0)

    win_ref[...] = jnp.zeros_like(win_ref)
    part(2, rows - EDGE, up_ref)
    part(0, 0, down_ref)


def merge_kernel(
    ids_ref, count_ref, info_ref, cols_ref, offs_ref, feat_ref, low_ref, high_ref, out_ref,
    tmp_ref, side_ref, win_ref, all_ref,
):
    frames, rows = feat_ref.shape[0], feat_ref.shape[1]
    tmp_ref[...] = jnp.zeros_like(tmp_ref)
    win_ref[...] = jnp.zeros_like(win_ref)

    def slot(s, carry):
        block = ids_ref[1, s]
        here = pl.ds(pl.multiple_of(s * frames * MSG, 16), frames * MSG)
        side_ref[0] = low_ref[here, :].astype(F32)
        side_ref[1] = high_ref[here, :].astype(F32)
        own = EDGE * RAW
        for k in range(frames):
            row = offs_ref[k, block]
            win_ref[0:MSG, :] = side_ref[0, k * MSG : (k + 1) * MSG, :]
            window_rows(feat_ref, tmp_ref, win_ref, own, k, 0, rows, cols_ref[k, block] - 1)
            top = own + rows * RAW
            win_ref[top : top + MSG, :] = side_ref[1, k * MSG : (k + 1) * MSG, :]
            all_ref[k * CELLS : k * CELLS + 128, :] = win_ref[pl.ds(row * RAW, 128), :]
        end = frames * CELLS
        all_ref[end:SLOT, :] = jnp.zeros((SLOT - end, 128), F32)
        for k in range(frames):
            first = (info_ref[0] * rows + offs_ref[k, block] - WIN // 2).astype(F32)
            all_ref[end + k : end + k + 1, :] = jnp.full((1, 128), first, F32)
        for i in range(PIECES):
            out_ref[i, pl.ds(pl.multiple_of(s * PROWS, 16), PROWS), :] = all_ref[
                i * PROWS : (i + 1) * PROWS, :
            ].astype(BF16)
        return carry

    lax.fori_loop(0, count_ref[1], slot, 0)


def route_kernel(owner_ref, rank_ref, in_ref, out_ref):
    def step(b, carry):
        out_ref[b] = in_ref[owner_ref[b], pl.ds(pl.multiple_of(rank_ref[b] * PROWS, 16), PROWS), :]
        return carry

    lax.fori_loop(0, out_ref.shape[0], step, 0, unroll=8)


def nt(a, b):
    return lax.dot_general(a, b, (((1,), (1,)), ((), ())), preferred_element_type=F32)


def rms_scale(values, gain):
    return values * lax.rsqrt(jnp.mean(values * values, axis=-1, keepdims=True) + 1e-06) * gain


def refine_kernel(
    height, raw_ref, wconv_ref, query_ref, wcorr_ref, wfeat_ref, time_ref, start_ref, gain1_ref,
    wk_ref, wq_ref, wv_ref, wout_ref, gain2_ref, wup_ref, wdown_ref, out_ref,
    cells_ref, cols_ref, tok_ref,
):
    groups, per = raw_ref.shape[0] // SLOT, 4
    frames = groups * per
    step = pl.program_id(0)

    @pl.when(step == 0)
    def _():
        cells_ref[0 : groups * SLOT, :] = raw_ref[...].astype(F32)
        cells_ref[groups * SLOT :, :] = jnp.zeros_like(cells_ref[groups * SLOT :, :])
        line = lax.broadcasted_iota(jnp.int32, (128, 128), 0) // RAW
        line = line.astype(F32)
        feat = jnp.dot(query_ref[...], wfeat_ref[...], preferred_element_type=F32)
        for f in range(frames):
            base = (f // per) * SLOT + (f % per) * CELLS
            for a in range(3):
                for b in range(3):
                    at = base + a * RAW + b
                    cols_ref[f * 128 : (f + 1) * 128, (a * 3 + b) * 128 : (a * 3 + b + 1) * 128] = (
                        cells_ref[at : at + 128, :].astype(BF16)
                    )
        conv = jnp.dot(cols_ref[...], wconv_ref[...], preferred_element_type=F32)
        corr = []
        for f in range(frames):
            info = (f // per) * SLOT + per * CELLS + f % per
            row = line + cells_ref[info : info + 1, :]
            inside = (row >= 0) & (row < height)
            here = jnp.where(inside, conv[f * 128 : (f + 1) * 128], 0.0).astype(BF16)
            corr.append((nt(query_ref[...], here) * (128 ** -0.5)).astype(BF16))
        tokens = jnp.dot(
            jnp.concatenate(corr, axis=0), wcorr_ref[...], preferred_element_type=F32
        )
        for f in range(frames):
            here = tokens[f * 128 : (f + 1) * 128] + feat + time_ref[f : f + 1, :]
            for part in range(3):
                tok_ref[part, pl.ds(f, 128, stride=frames), :] = here[
                    :, part * 128 : (part + 1) * 128
                ]

    here = pl.ds(pl.multiple_of(step * CHUNK, CHUNK), CHUNK)
    tokens = jnp.concatenate([tok_ref[part, here, :] for part in range(3)], axis=1)
    normed = rms_scale(tokens, gain1_ref[...]).astype(BF16)
    keys = jnp.dot(normed, wk_ref[...], preferred_element_type=F32).astype(BF16)
    query = nt(wq_ref[...], normed).astype(BF16)
    values = nt(wv_ref[...], normed).astype(BF16)
    track = lax.broadcasted_iota(jnp.int32, (16, 128), 1) // frames
    frame = lax.broadcasted_iota(jnp.int32, (16, 128), 0)
    key_track = lax.broadcasted_iota(jnp.int32, (128, 128), 0) // frames
    query_track = lax.broadcasted_iota(jnp.int32, (128, 128), 1) // frames
    same = (key_track == query_track).astype(BF16)
    factor = HEAD ** -0.5 * 1.4426950408889634
    zeros16 = jnp.zeros((16, 128), BF16)
    zeros64 = jnp.zeros((64, 128), BF16)
    attended = []
    for first in range(0, CHUNK // 128, BATCH):
        some = range(first, first + BATCH)
        own, valid = [], []
        for g in some:
            lanes = slice(g * 128, (g + 1) * 128)
            valid += [frame >= start_ref[0, :, lanes]] * HEADS
            for pair in range(HEADS // 2):
                one = query[2 * pair * HEAD : (2 * pair + 1) * HEAD, lanes]
                two = query[(2 * pair + 1) * HEAD : (2 * pair + 2) * HEAD, lanes]
                both = jnp.concatenate(
                    [
                        jnp.concatenate([one, zeros16, zeros64], axis=0),
                        jnp.concatenate([zeros64, two, zeros16], axis=0),
                    ],
                    axis=1,
                )
                scores = jnp.dot(
                    keys[lanes, pair * 128 : (pair + 1) * 128], both, preferred_element_type=F32
                )
                for h in range(2):
                    full = scores[:, h * 128 : (h + 1) * 128]
                    part = full[0:16, :]
                    for t in range(1, 8):
                        part = jnp.where(track == t, full[16 * t : 16 * (t + 1), :], part)
                    own.append(part)
        own = [jnp.where(v, p, -1e30) for v, p in zip(valid, own)]
        top = [jnp.max(p, axis=0, keepdims=True) for p in own]
        weights = [jnp.exp2((p - t) * factor) for p, t in zip(own, top)]
        total = [jnp.sum(w, axis=0, keepdims=True) for w in weights]
        probs = [(w * (1.0 / t)).astype(BF16) for w, t in zip(weights, total)]
        for g in some:
            lanes = slice(g * 128, (g + 1) * 128)
            heads = []
            for pair in range(HEADS // 2):
                two = [
                    jnp.concatenate([probs[(g - first) * HEADS + 2 * pair + h]] * 8, axis=0) * same
                    for h in range(2)
                ]
                at = 2 * pair * HEAD
                both = jnp.dot(
                    values[at : at + 2 * HEAD, lanes],
                    jnp.concatenate(two, axis=1),
                    preferred_element_type=F32,
                )
                heads += [both[:HEAD, :128], both[HEAD:, 128:]]
            attended.append(jnp.concatenate(heads, axis=0).T.astype(BF16))
    attended = jnp.concatenate(attended, axis=0)
    mixed = tokens + jnp.dot(attended, wout_ref[...], preferred_element_type=F32)
    normed2 = rms_scale(mixed, gain2_ref[...]).astype(BF16)
    hidden = jax.nn.gelu(
        jnp.dot(normed2, wup_ref[...], preferred_element_type=F32), approximate=True
    ).astype(BF16)
    result = mixed + jnp.dot(hidden, wdown_ref[...], preferred_element_type=F32)
    out_ref[...] = result.astype(BF16)


def params(mib):
    return pltpu.CompilerParams(vmem_limit_bytes=mib << 20)


SMEM = pl.BlockSpec(memory_space=pltpu.SMEM)
VMEM = pl.BlockSpec(memory_space=pltpu.VMEM)


def refine_call(height, raw, *rest):
    tokens, dim = rest[5].size, rest[4].shape[1]
    chans = raw.shape[1]
    step = pl.BlockSpec((1, 1, CHUNK), lambda i: (i, 0, 0))
    return pl.pallas_call(
        functools.partial(refine_kernel, height),
        grid=(tokens // CHUNK,),
        out_shape=jax.ShapeDtypeStruct((tokens, dim), BF16),
        in_specs=[VMEM] * 6 + [step] + [VMEM] * (len(rest) - 6),
        out_specs=pl.BlockSpec((CHUNK, dim), lambda i: (i, 0)),
        scratch_shapes=[
            pltpu.VMEM((raw.shape[0] + 16, 128), F32),
            pltpu.VMEM((tokens, 9 * chans), BF16),
            pltpu.VMEM((3, tokens, 128), F32),
        ],
        compiler_params=params(48),
        name="refine",
    )(raw, *rest)


def body(
    features, w_conv, query_feats, offset_rows, offset_cols, owners, start_frames, w_corr, w_feat,
    time_embed, gain_attn, w_qkv, w_attn_out, gain_mlp, w_up, w_down,
):
    n_tiles = lax.axis_size("tiles")
    tile = lax.axis_index("tiles")
    frames, rows, width, chans = features.shape
    blocks = owners.shape[0]
    tracks = query_feats.shape[0]
    total = time_embed.shape[0]
    dim = w_feat.shape[1]

    owner = owners[:, 0]
    number = jnp.arange(blocks, dtype=jnp.int32)
    rank = jnp.sum(
        (owner[:, None] == owner[None, :]) & (number[None, :] < number[:, None]), axis=1, dtype=jnp.int32
    )
    near = tile + jnp.arange(-1, 2, dtype=jnp.int32)
    mine = owner[None, :] == near[:, None]
    count = jnp.sum(mine, axis=1, dtype=jnp.int32)
    slots = jnp.arange(CAP, dtype=jnp.int32)
    ids = jnp.sum(
        jnp.where(mine[:, None, :] & (rank[None, None, :] == slots[None, :, None]), number, 0),
        axis=2,
        dtype=jnp.int32,
    )

    message = jax.ShapeDtypeStruct((CAP * frames * MSG, chans), BF16)
    up, down = pl.pallas_call(
        edge_kernel,
        out_shape=(message, message),
        in_specs=[SMEM, SMEM, SMEM, VMEM],
        out_specs=(VMEM, VMEM),
        scratch_shapes=[pltpu.VMEM((TILE, 48, 128), F32), pltpu.VMEM((frames * MSG + 16, 128), F32)],
        compiler_params=params(24),
        name="edges",
    )(ids, count, offset_cols, features)
    low = lax.ppermute(up, "tiles", [(i, i + 1) for i in range(n_tiles - 1)])
    high = lax.ppermute(down, "tiles", [(i + 1, i) for i in range(n_tiles - 1)])
    pieces = pl.pallas_call(
        merge_kernel,
        out_shape=jax.ShapeDtypeStruct((PIECES, CAP * PROWS, chans), BF16),
        in_specs=[SMEM, SMEM, SMEM, SMEM, SMEM, VMEM, VMEM, VMEM],
        out_specs=VMEM,
        scratch_shapes=[
            pltpu.VMEM((TILE, 48, 128), F32),
            pltpu.VMEM((2, frames * MSG, 128), F32),
            pltpu.VMEM((208, 128), F32),
            pltpu.VMEM((SLOT, 128), F32),
        ],
        compiler_params=params(24),
        name="windows",
    )(ids, count, tile.reshape(1), offset_cols, offset_rows, features, low, high)
    spread = lax.all_to_all(pieces, "tiles", 0, 0, tiled=True)
    routed = pl.pallas_call(
        route_kernel,
        out_shape=jax.ShapeDtypeStruct((blocks, PROWS, chans), BF16),
        in_specs=[SMEM, SMEM, VMEM],
        out_specs=VMEM,
        compiler_params=params(24),
        name="route",
    )(owner, rank, spread)
    raw = lax.all_to_all(routed, ("frames", "tiles"), 0, 0, tiled=True)
    raw = raw.reshape(blocks * PROWS, chans)

    wk = jnp.pad(w_qkv[:, dim : 2 * dim].reshape(dim, HEADS, HEAD), ((0, 0), (0, 0), (0, 16)))
    wk = wk.reshape(dim, HEADS * 64)
    wq, wv = w_qkv[:, :dim].T, w_qkv[:, 2 * dim :].T
    wcorr = jnp.pad(w_corr.reshape(WIN, WIN, dim), ((0, 0), (0, RAW - WIN), (0, 0)))
    wcorr = jnp.pad(wcorr.reshape(WIN * RAW, dim), ((0, 128 - WIN * RAW), (0, 0)))
    tokens = tracks * total
    start = jnp.repeat(start_frames, total).reshape(tokens // CHUNK, 1, CHUNK)
    refined = refine_call(
        n_tiles * rows, raw, w_conv.reshape(9 * chans, chans), query_feats, wcorr, w_feat, time_embed,
        start, gain_attn.reshape(1, dim), wk, wq, wv, w_attn_out, gain_mlp.reshape(1, dim), w_up, w_down,
    )
    return refined.reshape(tracks, total, dim)


def solution(mesh):
    placed = (
        P("frames", "tiles", None, None),
        P(),
        P(("frames", "tiles"), None),
        P("frames", None),
        P("frames", None),
        P(),
        P(("frames", "tiles")),
        P(), P(), P(), P(), P(), P(), P(), P(), P(),
    )
    return jax.shard_map(
        body,
        mesh=mesh,
        in_specs=placed,
        out_specs=P(("frames", "tiles"), None, None),
        check_vma=False,
    )
```

```python
import functools

import jax
import jax.numpy as jnp
from jax import lax
from jax.experimental import pallas as pl
from jax.experimental.pallas import tpu as pltpu
from jax.sharding import PartitionSpec as P

HEADS = 8
HEAD = 48
WIN = 9
RAW = WIN + 2
CELLS = RAW * RAW
QBLK = 128
CAP = 12
TILE = 8
EDGE = 5
MSG = 56
PIECES = 32
PROWS = 16
SLOT = PIECES * PROWS
CHUNK = 1024
BATCH = 4
F32 = jnp.float32
BF16 = jnp.bfloat16


def aligned(col, wide):
    return pl.multiple_of(jnp.clip((col >> 4) << 4, 0, wide - 32), 16)


def window_rows(source, rows, shift, tmp_ref, dst_ref, base):
    tmp_ref[0:rows, 8:40, :] = source.astype(F32)
    for i in range(rows):
        dst_ref[base + RAW * i : base + RAW * i + 16, :] = tmp_ref[i, pl.ds(8 + shift, 16), :]


def edge_kernel(
    owners_ref, cols_ref, feat_ref, pair_ref, cross_ref, ids_ref, buf_ref, tmp_ref, win_ref, sems
):
    frames, rows, wide, _ = feat_ref.shape
    tile = lax.axis_index("tiles")

    def scan(b, counts):
        near = owners_ref[b] - tile + 1
        for d in range(3):
            ids_ref[16 * d + counts[d]] = b
        return tuple(counts[d] + (near == d).astype(jnp.int32) for d in range(3))

    zero = jnp.int32(0)
    counts = lax.fori_loop(0, owners_ref.shape[0], scan, (zero, zero, zero), unroll=8)
    for d in range(3):
        ids_ref[48 + d] = counts[d]
    odd = tile & 1
    parts = []
    for w, after in ((0, odd), (1, 1 - odd)):
        first = jnp.where(after == 1, rows - EDGE, 0)
        parts.append((w, 32 * after, ids_ref[48 + 2 * after], first))

    def copy(w, s, k, first, block):
        start = aligned(cols_ref[k, block] - 1, wide)
        return pltpu.make_async_copy(
            feat_ref.at[k, pl.ds(first, EDGE), pl.ds(start, 32), :], buf_ref.at[w, s, k], sems.at[w, s, k]
        )

    for w, at, count, first in parts:

        def begin(s, carry):
            for k in range(frames):
                copy(w, s, k, first, ids_ref[at + s]).start()
            return carry

        lax.fori_loop(0, count, begin, 0)
    tmp_ref[...] = jnp.zeros_like(tmp_ref)
    win_ref[...] = jnp.zeros_like(win_ref)
    for w, at, count, first in parts:
        out_ref = (cross_ref, pair_ref)[w]

        def slot(s, carry):
            block = ids_ref[at + s]
            for k in range(frames):
                copy(w, s, k, first, block).wait()
                col = cols_ref[k, block] - 1
                window_rows(buf_ref[w, s, k], EDGE, col - aligned(col, wide), tmp_ref, win_ref, k * MSG)
            out_ref[pl.ds(pl.multiple_of(s * frames * MSG, 16), frames * MSG), :] = win_ref[
                0 : frames * MSG, :
            ].astype(BF16)
            return carry

        lax.fori_loop(0, count, slot, 0)


def merge_kernel(
    ids_ref, cols_ref, offs_ref, feat_ref, pair_ref, cross_ref, out_ref, tmp_ref, side_ref, win_ref, all_ref
):
    frames, rows, wide, _ = feat_ref.shape
    tile = lax.axis_index("tiles")
    odd = tile & 1
    tmp_ref[...] = jnp.zeros_like(tmp_ref)
    win_ref[...] = jnp.zeros_like(win_ref)

    def slot(s, carry):
        block = ids_ref[16 + s]
        here = pl.ds(pl.multiple_of(s * frames * MSG, 16), frames * MSG)
        side_ref[odd] = cross_ref[here, :].astype(F32)
        side_ref[1 - odd] = pair_ref[here, :].astype(F32)
        own = EDGE * RAW
        for k in range(frames):
            row, col = offs_ref[k, block], cols_ref[k, block] - 1
            win_ref[0:MSG, :] = side_ref[0, k * MSG : (k + 1) * MSG, :]
            start = aligned(col, wide)
            window_rows(feat_ref[k, :, pl.ds(start, 32), :], rows, col - start, tmp_ref, win_ref, own)
            top = own + rows * RAW
            win_ref[top : top + MSG, :] = side_ref[1, k * MSG : (k + 1) * MSG, :]
            all_ref[k * CELLS : k * CELLS + 128, :] = win_ref[pl.ds(row * RAW, 128), :]
        end = frames * CELLS
        all_ref[end:SLOT, :] = jnp.zeros((SLOT - end, 128), F32)
        for k in range(frames):
            first = (tile * rows + offs_ref[k, block] - WIN // 2).astype(F32)
            all_ref[end + k : end + k + 1, :] = jnp.full((1, 128), first, F32)
        for i in range(PIECES):
            out_ref[i, pl.ds(pl.multiple_of(s * PROWS, 16), PROWS), :] = all_ref[
                i * PROWS : (i + 1) * PROWS, :
            ].astype(BF16)
        return carry

    lax.fori_loop(0, ids_ref[49], slot, 0)


def route_kernel(index_ref, in_ref, out_ref):
    def step(b, carry):
        out_ref[b] = in_ref[index_ref[b]]
        return carry

    lax.fori_loop(0, out_ref.shape[0], step, 0, unroll=16)


def nt(a, b):
    return lax.dot_general(a, b, (((1,), (1,)), ((), ())), preferred_element_type=F32)


def rms_scale(values, gain):
    return values * lax.rsqrt(jnp.mean(values * values, axis=-1, keepdims=True) + 1e-06) * gain


def refine_kernel(
    height, raw_ref, wconv_ref, query_ref, wcorr_ref, wfeat_ref, time_ref, start_ref, gain1_ref,
    wk_ref, wq_ref, wv_ref, wout_ref, gain2_ref, wup_ref, wdown_ref, out_ref,
    cells_ref, cols_ref, tok_ref, down_ref, sem,
):
    groups, per = raw_ref.shape[0] // SLOT, 4
    frames = groups * per
    step = pl.program_id(0)

    @pl.when(step == 0)
    def _():
        fetch = pltpu.make_async_copy(wdown_ref, down_ref, sem)
        fetch.start()
        cells_ref[0 : groups * SLOT, :] = raw_ref[...].astype(F32)
        cells_ref[groups * SLOT :, :] = jnp.zeros_like(cells_ref[groups * SLOT :, :])
        line = lax.broadcasted_iota(jnp.int32, (128, 128), 0) // RAW
        line = line.astype(F32)
        feat = jnp.dot(query_ref[...], wfeat_ref[...], preferred_element_type=F32)
        for f in range(frames):
            base = (f // per) * SLOT + (f % per) * CELLS
            for a in range(3):
                for b in range(3):
                    at = base + a * RAW + b
                    cols_ref[f * 128 : (f + 1) * 128, (a * 3 + b) * 128 : (a * 3 + b + 1) * 128] = (
                        cells_ref[at : at + 128, :].astype(BF16)
                    )
        conv = jnp.dot(cols_ref[...], wconv_ref[...], preferred_element_type=F32)
        corr = []
        for f in range(frames):
            info = (f // per) * SLOT + per * CELLS + f % per
            row = line + cells_ref[info : info + 1, :]
            inside = (row >= 0) & (row < height)
            here = jnp.where(inside, conv[f * 128 : (f + 1) * 128], 0.0).astype(BF16)
            corr.append((nt(query_ref[...], here) * (128 ** -0.5)).astype(BF16))
        tokens = jnp.dot(
            jnp.concatenate(corr, axis=0), wcorr_ref[...], preferred_element_type=F32
        )
        for f in range(frames):
            here = tokens[f * 128 : (f + 1) * 128] + feat + time_ref[f : f + 1, :]
            for part in range(3):
                tok_ref[part, pl.ds(f, 128, stride=frames), :] = here[
                    :, part * 128 : (part + 1) * 128
                ]
        fetch.wait()

    here = pl.ds(pl.multiple_of(step * CHUNK, CHUNK), CHUNK)
    tokens = jnp.concatenate([tok_ref[part, here, :] for part in range(3)], axis=1)
    normed = rms_scale(tokens, gain1_ref[...]).astype(BF16)
    keys = jnp.dot(normed, wk_ref[...], preferred_element_type=F32).astype(BF16)
    query = nt(wq_ref[...], normed).astype(BF16)
    values = nt(wv_ref[...], normed).astype(BF16)
    track = lax.broadcasted_iota(jnp.int32, (16, 128), 1) // frames
    frame = lax.broadcasted_iota(jnp.int32, (16, 128), 0)
    key_track = lax.broadcasted_iota(jnp.int32, (128, 128), 0) // frames
    query_track = lax.broadcasted_iota(jnp.int32, (128, 128), 1) // frames
    same = (key_track == query_track).astype(BF16)
    factor = HEAD ** -0.5 * 1.4426950408889634
    zeros16 = jnp.zeros((16, 128), BF16)
    zeros64 = jnp.zeros((64, 128), BF16)
    attended = []
    for first in range(0, CHUNK // 128, BATCH):
        some = range(first, first + BATCH)
        own, valid = [], []
        for g in some:
            lanes = slice(g * 128, (g + 1) * 128)
            valid += [frame >= start_ref[0, :, lanes]] * HEADS
            for pair in range(HEADS // 2):
                one = query[2 * pair * HEAD : (2 * pair + 1) * HEAD, lanes]
                two = query[(2 * pair + 1) * HEAD : (2 * pair + 2) * HEAD, lanes]
                both = jnp.concatenate(
                    [
                        jnp.concatenate([one, zeros16, zeros64], axis=0),
                        jnp.concatenate([zeros64, two, zeros16], axis=0),
                    ],
                    axis=1,
                )
                scores = jnp.dot(
                    keys[lanes, pair * 128 : (pair + 1) * 128], both, preferred_element_type=F32
                )
                for h in range(2):
                    full = scores[:, h * 128 : (h + 1) * 128]
                    part = full[0:16, :]
                    for t in range(1, 8):
                        part = jnp.where(track == t, full[16 * t : 16 * (t + 1), :], part)
                    own.append(part)
        own = [jnp.where(v, p, -1e30) for v, p in zip(valid, own)]
        top = [jnp.max(p, axis=0, keepdims=True) for p in own]
        weights = [jnp.exp2((p - t) * factor) for p, t in zip(own, top)]
        total = [jnp.sum(w, axis=0, keepdims=True) for w in weights]
        probs = [(w * (1.0 / t)).astype(BF16) for w, t in zip(weights, total)]
        for g in some:
            lanes = slice(g * 128, (g + 1) * 128)
            heads = []
            for pair in range(HEADS // 2):
                two = [
                    jnp.concatenate([probs[(g - first) * HEADS + 2 * pair + h]] * 8, axis=0) * same
                    for h in range(2)
                ]
                at = 2 * pair * HEAD
                both = jnp.dot(
                    values[at : at + 2 * HEAD, lanes],
                    jnp.concatenate(two, axis=1),
                    preferred_element_type=F32,
                )
                heads += [both[:HEAD, :128], both[HEAD:, 128:]]
            attended.append(jnp.concatenate(heads, axis=0).astype(BF16).T)
    attended = jnp.concatenate(attended, axis=0)
    mixed = tokens + jnp.dot(attended, wout_ref[...], preferred_element_type=F32)
    normed2 = rms_scale(mixed, gain2_ref[...]).astype(BF16)
    hidden = jax.nn.gelu(
        jnp.dot(normed2, wup_ref[...], preferred_element_type=F32), approximate=True
    ).astype(BF16)
    result = mixed + jnp.dot(hidden, down_ref[...], preferred_element_type=F32)
    out_ref[...] = result.astype(BF16)


def params(mib):
    return pltpu.CompilerParams(vmem_limit_bytes=mib << 20)


SMEM = pl.BlockSpec(memory_space=pltpu.SMEM)
VMEM = pl.BlockSpec(memory_space=pltpu.VMEM)
HBM = pl.BlockSpec(memory_space=pltpu.HBM)


def refine_call(height, raw, *rest):
    tokens, dim = rest[5].size, rest[4].shape[1]
    chans = raw.shape[1]
    step = pl.BlockSpec((1, 1, CHUNK), lambda i: (i, 0, 0))
    return pl.pallas_call(
        functools.partial(refine_kernel, height),
        grid=(tokens // CHUNK,),
        out_shape=jax.ShapeDtypeStruct((tokens, dim), BF16),
        in_specs=[VMEM] * 6 + [step] + [VMEM] * (len(rest) - 7) + [HBM],
        out_specs=pl.BlockSpec((CHUNK, dim), lambda i: (i, 0)),
        scratch_shapes=[
            pltpu.VMEM((raw.shape[0] + 16, 128), F32),
            pltpu.VMEM((tokens, 9 * chans), BF16),
            pltpu.VMEM((3, tokens, 128), F32),
            pltpu.VMEM(rest[-1].shape, BF16),
            pltpu.SemaphoreType.DMA,
        ],
        compiler_params=params(32),
        name="refine",
    )(raw, *rest[:-1], pltpu.with_memory_space_constraint(rest[-1], pltpu.HBM))


def body(
    features, w_conv, query_feats, offset_rows, offset_cols, owners, start_frames, w_corr, w_feat,
    time_embed, gain_attn, w_qkv, w_attn_out, gain_mlp, w_up, w_down,
):
    n_tiles = lax.axis_size("tiles")
    frames, rows, width, chans = features.shape
    blocks = owners.shape[0]
    tracks = query_feats.shape[0]
    total = time_embed.shape[0]
    dim = w_feat.shape[1]

    owner = owners[:, 0]
    number = jnp.arange(blocks, dtype=jnp.int32)
    rank = jnp.sum(
        (owner[:, None] == owner[None, :]) & (number[None, :] < number[:, None]), axis=1, dtype=jnp.int32
    )
    message = jax.ShapeDtypeStruct((CAP * frames * MSG, chans), BF16)
    pair, cross, ids = pl.pallas_call(
        edge_kernel,
        out_shape=(message, message, jax.ShapeDtypeStruct((64,), jnp.int32)),
        in_specs=[SMEM, SMEM, HBM],
        out_specs=(VMEM, VMEM, SMEM),
        scratch_shapes=[
            pltpu.VMEM((2, CAP, frames, EDGE, 32, chans), BF16),
            pltpu.VMEM((TILE, 48, 128), F32),
            pltpu.VMEM((frames * MSG + 16, 128), F32),
            pltpu.SemaphoreType.DMA((2, CAP, frames)),
        ],
        compiler_params=params(24),
        name="edges",
    )(owner, offset_cols, pltpu.with_memory_space_constraint(features, pltpu.HBM))
    beside = [(i, ((i - 1) ^ 1) + 1) for i in range(1, n_tiles - 1)]
    cross = lax.ppermute(cross, "tiles", beside)
    pair = lax.ppermute(pair, "tiles", [(i, i ^ 1) for i in range(n_tiles)])
    pieces = pl.pallas_call(
        merge_kernel,
        out_shape=jax.ShapeDtypeStruct((PIECES, CAP * PROWS, chans), BF16),
        in_specs=[SMEM, SMEM, SMEM, VMEM, VMEM, VMEM],
        out_specs=VMEM,
        scratch_shapes=[
            pltpu.VMEM((TILE, 48, 128), F32),
            pltpu.VMEM((2, frames * MSG, 128), F32),
            pltpu.VMEM((208, 128), F32),
            pltpu.VMEM((SLOT, 128), F32),
        ],
        compiler_params=params(24),
        name="windows",
    )(ids, offset_cols, offset_rows, features, pair, cross)
    spread = lax.all_to_all(pieces, "tiles", 0, 0, tiled=True)
    routed = pl.pallas_call(
        route_kernel,
        out_shape=jax.ShapeDtypeStruct((blocks, PROWS, chans), BF16),
        in_specs=[SMEM, VMEM],
        out_specs=VMEM,
        compiler_params=params(24),
        name="route",
    )(owner * CAP + rank, spread.reshape(n_tiles * CAP, PROWS, chans))
    raw = lax.all_to_all(routed, ("frames", "tiles"), 0, 0, tiled=True)
    raw = raw.reshape(blocks * PROWS, chans)

    wk = jnp.pad(w_qkv[:, dim : 2 * dim].reshape(dim, HEADS, HEAD), ((0, 0), (0, 0), (0, 16)))
    wk = wk.reshape(dim, HEADS * 64)
    wq, wv = w_qkv[:, :dim].T, w_qkv[:, 2 * dim :].T
    wcorr = jnp.pad(w_corr.reshape(WIN, WIN, dim), ((0, 0), (0, RAW - WIN), (0, 0)))
    wcorr = jnp.pad(wcorr.reshape(WIN * RAW, dim), ((0, 128 - WIN * RAW), (0, 0)))
    tokens = tracks * total
    start = jnp.repeat(start_frames, total).reshape(tokens // CHUNK, 1, CHUNK)
    refined = refine_call(
        n_tiles * rows, raw, w_conv.reshape(9 * chans, chans), query_feats, wcorr, w_feat, time_embed,
        start, gain_attn.reshape(1, dim), wk, wq, wv, w_attn_out, gain_mlp.reshape(1, dim), w_up, w_down,
    )
    return refined.reshape(tracks, total, dim)


def solution(mesh):
    placed = (
        P("frames", "tiles", None, None),
        P(),
        P(("frames", "tiles"), None),
        P("frames", None),
        P("frames", None),
        P(),
        P(("frames", "tiles")),
        P(), P(), P(), P(), P(), P(), P(), P(), P(),
    )
    return jax.shard_map(
        body,
        mesh=mesh,
        in_specs=placed,
        out_specs=P(("frames", "tiles"), None, None),
        check_vma=False,
    )
```

```python
import functools

import jax
import jax.numpy as jnp
from jax import lax
from jax.experimental import pallas as pl
from jax.experimental.pallas import tpu as pltpu
from jax.sharding import PartitionSpec as P

HEADS = 8
HEAD = 48
WIN = 9
RAW = WIN + 2
QBLK = 128
CAP = 12
TILE = 8
EDGE = 5
CLASSES = 8
PIECES = 32
PROWS = 16
OWN = 11
SIDE = 7
LOW = CAP * OWN
HIGH = LOW + CAP * SIDE
SENT = 304
CHUNK = 1024
BATCH = 4
F32 = jnp.float32
BF16 = jnp.bfloat16


def aligned(col, wide):
    return pl.multiple_of(jnp.clip((col >> 4) << 4, 0, wide - 32), 16)


def window_rows(source, rows, shift, tmp_ref, dst_ref, base):
    tmp_ref[0:rows, 8:40, :] = source.astype(F32)
    for i in range(rows):
        dst_ref[base + RAW * i : base + RAW * i + 16, :] = tmp_ref[i, pl.ds(8 + shift, 16), :]


def first_of(cell, which):
    return (cell - which + CLASSES - 1) >> 3


def send_kernel(
    owners_ref, cols_ref, offs_ref, feat_ref, out_ref, here_ref, ids_ref, tmp_ref, flat_ref, piece_ref, sems
):
    frames, rows, wide, _ = feat_ref.shape
    tile = lax.axis_index("tiles")
    copies = [pltpu.make_async_copy(feat_ref.at[k], here_ref.at[k], sems.at[k]) for k in range(frames)]
    for copy in copies:
        copy.start()

    def scan(b, counts):
        near = owners_ref[b] - tile + 1
        for d in range(3):
            ids_ref[16 * d + counts[d]] = b
        return tuple(counts[d] + (near == d).astype(jnp.int32) for d in range(3))

    zero = jnp.int32(0)
    counts = lax.fori_loop(0, owners_ref.shape[0], scan, (zero, zero, zero), unroll=8)
    tmp_ref[...] = jnp.zeros_like(tmp_ref)
    flat_ref[...] = jnp.zeros_like(flat_ref)
    for k in range(frames):
        copies[k].wait()

        def part(d, row0, count, place, room, k=k):
            def slot(s, carry):
                block = ids_ref[16 * d + s]
                row, col = offs_ref[k, block], cols_ref[k, block] - 1
                start = aligned(col, wide)
                window_rows(
                    here_ref[k, row0 : row0 + count, pl.ds(start, 32), :], count, col - start, tmp_ref, flat_ref, 16
                )
                at = RAW * (EDGE - row + row0 + (rows, 0, -rows)[d])
                low = jnp.maximum(at, 0)
                for c in range(CLASSES):
                    source = 16 + CLASSES * first_of(low, c) + c - at
                    target = (k * CLASSES + c) * SENT + place + s * room
                    length = 16 if d == 1 else 8
                    piece_ref[pl.ds(target, length), :] = flat_ref[pl.ds(source, length, stride=CLASSES), :]
                return carry

            lax.fori_loop(0, counts[d], slot, 0)

        part(1, 0, rows, 0, OWN)
        part(2, rows - EDGE, EDGE, LOW, SIDE)
        part(0, 0, EDGE, HIGH, SIDE)

    def narrow(i, carry):
        out_ref[i] = piece_ref[pl.ds(pl.multiple_of(i * SENT, 16), SENT), :].astype(BF16)
        return carry

    lax.fori_loop(0, PIECES, narrow, 0)


def route_kernel(height, owner_ref, rank_ref, offs_ref, in_ref, out_ref, wide_ref, join_ref):
    tiles = in_ref.shape[0]
    rows = height // tiles
    piece = lax.axis_index("tiles")
    frame, which = piece >> 3, piece & 7

    def widen(i, carry):
        wide_ref[pl.ds(pl.multiple_of(i * SENT, 16), SENT), :] = in_ref[i].astype(F32)
        return carry

    lax.fori_loop(0, tiles, widen, 0)
    none = tiles * SENT
    wide_ref[none:, :] = jnp.zeros_like(wide_ref[none:, :])
    last = jnp.where(which > 0, PROWS - 1, 24)

    def gather(b, carry):
        owner, slot, row = owner_ref[b], rank_ref[b], offs_ref[frame, b]
        before = jnp.where(owner > 0, (owner - 1) * SENT + LOW + slot * SIDE, none)
        after = jnp.where(owner < tiles - 1, (owner + 1) * SENT + HIGH + slot * SIDE, none)
        own = first_of(RAW * jnp.maximum(EDGE - row, 0), which)
        over = first_of(RAW * (EDGE + rows - row), which)
        join_ref[b, 0:8, :] = wide_ref[pl.ds(before, 8), :]
        join_ref[b, pl.ds(own, 16), :] = wide_ref[pl.ds(owner * SENT + slot * OWN, 16), :]
        join_ref[b, pl.ds(over, 8), :] = wide_ref[pl.ds(after, 8), :]
        top = (owner * rows + row - WIN // 2).astype(F32)
        join_ref[b, pl.ds(last, 1), :] = jnp.full((1, 128), top, F32)
        return carry

    lax.fori_loop(0, out_ref.shape[0], gather, 0, unroll=4)

    def narrow(b, carry):
        out_ref[b] = join_ref[b, 0:PROWS, :].astype(BF16)
        return carry

    lax.fori_loop(0, out_ref.shape[0], narrow, 0, unroll=8)


def nt(a, b):
    return lax.dot_general(a, b, (((1,), (1,)), ((), ())), preferred_element_type=F32)


def rms_scale(values, gain):
    return values * lax.rsqrt(jnp.mean(values * values, axis=-1, keepdims=True) + 1e-06) * gain


def refine_kernel(
    height, raw_ref, wconv_ref, query_ref, wcorr_ref, wfeat_ref, time_ref, start_ref, gain1_ref,
    wk_ref, wq_ref, wv_ref, wout_ref, gain2_ref, wup_ref, wdown_ref, out_ref,
    cells_ref, cols_ref, tok_ref, down_ref, sem,
):
    frames = raw_ref.shape[0] // 128
    step = pl.program_id(0)

    @pl.when(step == 0)
    def _():
        fetch = pltpu.make_async_copy(wdown_ref, down_ref, sem)
        fetch.start()
        for f in range(frames):
            for c in range(CLASSES):
                at = (f * CLASSES + c) * PROWS
                cells_ref[pl.ds(f * 128 + c, PROWS, stride=CLASSES), :] = raw_ref[at : at + PROWS, :].astype(F32)
        cells_ref[frames * 128 :, :] = jnp.zeros_like(cells_ref[frames * 128 :, :])
        line = lax.broadcasted_iota(jnp.int32, (128, 128), 0) // RAW
        line = line.astype(F32)
        feat = jnp.dot(query_ref[...], wfeat_ref[...], preferred_element_type=F32)
        for f in range(frames):
            for a in range(3):
                for b in range(3):
                    at = f * 128 + a * RAW + b
                    cols_ref[f * 128 : (f + 1) * 128, (a * 3 + b) * 128 : (a * 3 + b + 1) * 128] = (
                        cells_ref[at : at + 128, :].astype(BF16)
                    )
        conv = jnp.dot(cols_ref[...], wconv_ref[...], preferred_element_type=F32)
        corr = []
        for f in range(frames):
            info = f * 128 + 127
            row = line + cells_ref[info : info + 1, :]
            inside = (row >= 0) & (row < height)
            here = jnp.where(inside, conv[f * 128 : (f + 1) * 128], 0.0).astype(BF16)
            corr.append((nt(query_ref[...], here) * (128 ** -0.5)).astype(BF16))
        tokens = jnp.dot(
            jnp.concatenate(corr, axis=0), wcorr_ref[...], preferred_element_type=F32
        )
        for f in range(frames):
            here = tokens[f * 128 : (f + 1) * 128] + feat + time_ref[f : f + 1, :]
            for part in range(3):
                tok_ref[part, pl.ds(f, 128, stride=frames), :] = here[
                    :, part * 128 : (part + 1) * 128
                ]
        fetch.wait()

    here = pl.ds(pl.multiple_of(step * CHUNK, CHUNK), CHUNK)
    tokens = jnp.concatenate([tok_ref[part, here, :] for part in range(3)], axis=1)
    normed = rms_scale(tokens, gain1_ref[...]).astype(BF16)
    keys = jnp.dot(normed, wk_ref[...], preferred_element_type=F32).astype(BF16)
    query = nt(wq_ref[...], normed).astype(BF16)
    values = nt(wv_ref[...], normed).astype(BF16)
    track = lax.broadcasted_iota(jnp.int32, (16, 128), 1) // frames
    frame = lax.broadcasted_iota(jnp.int32, (16, 128), 0)
    key_track = lax.broadcasted_iota(jnp.int32, (128, 128), 0) // frames
    query_track = lax.broadcasted_iota(jnp.int32, (128, 128), 1) // frames
    same = (key_track == query_track).astype(BF16)
    factor = HEAD ** -0.5 * 1.4426950408889634
    zeros16 = jnp.zeros((16, 128), BF16)
    zeros64 = jnp.zeros((64, 128), BF16)
    attended = []
    for first in range(0, CHUNK // 128, BATCH):
        some = range(first, first + BATCH)
        own, valid = [], []
        for g in some:
            lanes = slice(g * 128, (g + 1) * 128)
            valid += [frame >= start_ref[0, :, lanes]] * HEADS
            for pair in range(HEADS // 2):
                one = query[2 * pair * HEAD : (2 * pair + 1) * HEAD, lanes]
                two = query[(2 * pair + 1) * HEAD : (2 * pair + 2) * HEAD, lanes]
                both = jnp.concatenate(
                    [
                        jnp.concatenate([one, zeros16, zeros64], axis=0),
                        jnp.concatenate([zeros64, two, zeros16], axis=0),
                    ],
                    axis=1,
                )
                scores = jnp.dot(
                    keys[lanes, pair * 128 : (pair + 1) * 128], both, preferred_element_type=F32
                )
                for h in range(2):
                    full = scores[:, h * 128 : (h + 1) * 128]
                    part = full[0:16, :]
                    for t in range(1, 8):
                        part = jnp.where(track == t, full[16 * t : 16 * (t + 1), :], part)
                    own.append(part)
        own = [jnp.where(v, p, -1e30) for v, p in zip(valid, own)]
        top = [jnp.max(p, axis=0, keepdims=True) for p in own]
        weights = [jnp.exp2((p - t) * factor) for p, t in zip(own, top)]
        total = [jnp.sum(w, axis=0, keepdims=True) for w in weights]
        probs = [(w * (1.0 / t)).astype(BF16) for w, t in zip(weights, total)]
        for g in some:
            lanes = slice(g * 128, (g + 1) * 128)
            heads = []
            for pair in range(HEADS // 2):
                two = [
                    jnp.concatenate([probs[(g - first) * HEADS + 2 * pair + h]] * 8, axis=0) * same
                    for h in range(2)
                ]
                at = 2 * pair * HEAD
                both = jnp.dot(
                    values[at : at + 2 * HEAD, lanes],
                    jnp.concatenate(two, axis=1),
                    preferred_element_type=F32,
                )
                heads += [both[:HEAD, :128], both[HEAD:, 128:]]
            attended.append(jnp.concatenate(heads, axis=0).astype(BF16).T)
    attended = jnp.concatenate(attended, axis=0)
    mixed = tokens + jnp.dot(attended, wout_ref[...], preferred_element_type=F32)
    normed2 = rms_scale(mixed, gain2_ref[...]).astype(BF16)
    hidden = jax.nn.gelu(
        jnp.dot(normed2, wup_ref[...], preferred_element_type=F32), approximate=True
    ).astype(BF16)
    result = mixed + jnp.dot(hidden, down_ref[...], preferred_element_type=F32)
    out_ref[...] = result.astype(BF16)


def params(mib):
    return pltpu.CompilerParams(vmem_limit_bytes=mib << 20)


SMEM = pl.BlockSpec(memory_space=pltpu.SMEM)
VMEM = pl.BlockSpec(memory_space=pltpu.VMEM)
HBM = pl.BlockSpec(memory_space=pltpu.HBM)


def refine_call(height, raw, *rest):
    tokens, dim = rest[5].size, rest[4].shape[1]
    chans = raw.shape[1]
    step = pl.BlockSpec((1, 1, CHUNK), lambda i: (i, 0, 0))
    return pl.pallas_call(
        functools.partial(refine_kernel, height),
        grid=(tokens // CHUNK,),
        out_shape=jax.ShapeDtypeStruct((tokens, dim), BF16),
        in_specs=[VMEM] * 6 + [step] + [VMEM] * (len(rest) - 7) + [HBM],
        out_specs=pl.BlockSpec((CHUNK, dim), lambda i: (i, 0)),
        scratch_shapes=[
            pltpu.VMEM((raw.shape[0] + 32, 128), F32),
            pltpu.VMEM((tokens, 9 * chans), BF16),
            pltpu.VMEM((3, tokens, 128), F32),
            pltpu.VMEM(rest[-1].shape, BF16),
            pltpu.SemaphoreType.DMA,
        ],
        compiler_params=params(32),
        name="refine",
    )(raw, *rest[:-1], pltpu.with_memory_space_constraint(rest[-1], pltpu.HBM))


def body(
    features, w_conv, query_feats, offset_rows, offset_cols, owners, start_frames, w_corr, w_feat,
    time_embed, gain_attn, w_qkv, w_attn_out, gain_mlp, w_up, w_down,
):
    n_tiles = lax.axis_size("tiles")
    frames, rows, width, chans = features.shape
    blocks = owners.shape[0]
    tracks = query_feats.shape[0]
    total = time_embed.shape[0]
    dim = w_feat.shape[1]

    owner = owners[:, 0]
    number = jnp.arange(blocks, dtype=jnp.int32)
    rank = jnp.sum(
        (owner[:, None] == owner[None, :]) & (number[None, :] < number[:, None]), axis=1, dtype=jnp.int32
    )
    pieces = pl.pallas_call(
        send_kernel,
        out_shape=jax.ShapeDtypeStruct((PIECES, SENT, chans), BF16),
        in_specs=[SMEM, SMEM, SMEM, HBM],
        out_specs=VMEM,
        scratch_shapes=[
            pltpu.VMEM(features.shape, BF16),
            pltpu.SMEM((64,), jnp.int32),
            pltpu.VMEM((TILE, 48, 128), F32),
            pltpu.VMEM((192, 128), F32),
            pltpu.VMEM((PIECES * SENT, 128), F32),
            pltpu.SemaphoreType.DMA((frames,)),
        ],
        compiler_params=params(32),
        name="windows",
    )(owner, offset_cols, offset_rows, pltpu.with_memory_space_constraint(features, pltpu.HBM))
    spread = lax.all_to_all(pieces, "tiles", 0, 0, tiled=True)
    routed = pl.pallas_call(
        functools.partial(route_kernel, n_tiles * rows),
        out_shape=jax.ShapeDtypeStruct((blocks, PROWS, chans), BF16),
        in_specs=[SMEM, SMEM, SMEM, VMEM],
        out_specs=VMEM,
        scratch_shapes=[
            pltpu.VMEM((n_tiles * SENT + 16, 128), F32),
            pltpu.VMEM((blocks, 32, 128), F32),
        ],
        compiler_params=params(32),
        name="route",
    )(owner, rank, offset_rows, spread)
    raw = lax.all_to_all(routed, ("frames", "tiles"), 0, 0, tiled=True)
    raw = raw.reshape(blocks * PROWS, chans)

    wk = jnp.pad(w_qkv[:, dim : 2 * dim].reshape(dim, HEADS, HEAD), ((0, 0), (0, 0), (0, 16)))
    wk = wk.reshape(dim, HEADS * 64)
    wq, wv = w_qkv[:, :dim].T, w_qkv[:, 2 * dim :].T
    wcorr = jnp.pad(w_corr.reshape(WIN, WIN, dim), ((0, 0), (0, RAW - WIN), (0, 0)))
    wcorr = jnp.pad(wcorr.reshape(WIN * RAW, dim), ((0, 128 - WIN * RAW), (0, 0)))
    tokens = tracks * total
    start = jnp.repeat(start_frames, total).reshape(tokens // CHUNK, 1, CHUNK)
    refined = refine_call(
        n_tiles * rows, raw, w_conv.reshape(9 * chans, chans), query_feats, wcorr, w_feat, time_embed,
        start, gain_attn.reshape(1, dim), wk, wq, wv, w_attn_out, gain_mlp.reshape(1, dim), w_up, w_down,
    )
    return refined.reshape(tracks, total, dim)


def solution(mesh):
    placed = (
        P("frames", "tiles", None, None),
        P(),
        P(("frames", "tiles"), None),
        P("frames", None),
        P("frames", None),
        P(),
        P(("frames", "tiles")),
        P(), P(), P(), P(), P(), P(), P(), P(), P(),
    )
    return jax.shard_map(
        body,
        mesh=mesh,
        in_specs=placed,
        out_specs=P(("frames", "tiles"), None, None),
        check_vma=False,
    )
```

```python
import functools

import jax
import jax.numpy as jnp
from jax import lax
from jax.experimental import pallas as pl
from jax.experimental.pallas import tpu as pltpu
from jax.sharding import PartitionSpec as P

HEADS = 8
HEAD = 48
WIN = 9
RAW = WIN + 2
QBLK = 128
CAP = 12
TILE = 8
EDGE = 5
CLASSES = 8
PIECES = 32
PROWS = 16
OWN = 11
SIDE = 7
LOW = CAP * OWN
HIGH = LOW + CAP * SIDE
SENT = 304
CHUNK = 1024
BATCH = 4
F32 = jnp.float32
BF16 = jnp.bfloat16


def aligned(col, wide):
    return pl.multiple_of(jnp.clip((col >> 4) << 4, 0, wide - 32), 16)


def window_rows(source, rows, shift, tmp_ref, dst_ref, base):
    tmp_ref[0:rows, 8:40, :] = source.astype(F32)
    for i in range(rows):
        dst_ref[base + RAW * i : base + RAW * i + 16, :] = tmp_ref[i, pl.ds(8 + shift, 16), :]


def first_of(cell, which):
    return (cell - which + CLASSES - 1) >> 3


def send_kernel(
    owners_hbm, cols_hbm, offs_hbm, feat_ref, out_ref, owners_ref, cols_ref, offs_ref, here_ref, ids_ref, tmp_ref,
    flat_ref, piece_ref, narrow_ref, table_sems, sems, out_sems,
):
    frames, rows, wide, _ = feat_ref.shape
    tile = lax.axis_index("tiles")
    tables = [
        pltpu.make_async_copy(source, target, table_sems.at[n])
        for n, (source, target) in enumerate(
            ((owners_hbm, owners_ref), (cols_hbm, cols_ref), (offs_hbm, offs_ref))
        )
    ]
    for copy in tables:
        copy.start()
    copies = [pltpu.make_async_copy(feat_ref.at[k], here_ref.at[k], sems.at[k]) for k in range(frames)]
    for copy in copies:
        copy.start()

    tmp_ref[...] = jnp.zeros_like(tmp_ref)
    flat_ref[...] = jnp.zeros_like(flat_ref)
    for copy in tables:
        copy.wait()

    def scan(b, counts):
        near = owners_ref[b] - tile + 1
        for d in range(3):
            ids_ref[16 * d + counts[d]] = b
        return tuple(counts[d] + (near == d).astype(jnp.int32) for d in range(3))

    zero = jnp.int32(0)
    counts = lax.fori_loop(0, owners_ref.shape[0], scan, (zero, zero, zero), unroll=8)

    def leave(i):
        return pltpu.make_async_copy(narrow_ref.at[i], out_ref.at[i], out_sems.at[i])

    for k in range(frames):
        copies[k].wait()

        def part(d, row0, count, place, room, k=k):
            def slot(s, carry):
                block = ids_ref[16 * d + s]
                row, col = offs_ref[k, block], cols_ref[k, block] - 1
                start = aligned(col, wide)
                window_rows(
                    here_ref[k, row0 : row0 + count, pl.ds(start, 32), :], count, col - start, tmp_ref, flat_ref, 16
                )
                at = RAW * (EDGE - row + row0 + (rows, 0, -rows)[d])
                low = jnp.maximum(at, 0)
                for c in range(CLASSES):
                    source = 16 + CLASSES * first_of(low, c) + c - at
                    target = (k * CLASSES + c) * SENT + place + s * room
                    length = 16 if d == 1 else 8
                    piece_ref[pl.ds(target, length), :] = flat_ref[pl.ds(source, length, stride=CLASSES), :]
                return carry

            lax.fori_loop(0, counts[d], slot, 0)

        part(1, 0, rows, 0, OWN)
        part(2, rows - EDGE, EDGE, LOW, SIDE)
        part(0, 0, EDGE, HIGH, SIDE)

        def narrow(i, carry):
            narrow_ref[i] = piece_ref[pl.ds(pl.multiple_of(i * SENT, 16), SENT), :].astype(BF16)
            leave(i).start()
            return carry

        lax.fori_loop(k * CLASSES, (k + 1) * CLASSES, narrow, 0)

    def wait(i, carry):
        leave(i).wait()
        return carry

    lax.fori_loop(0, PIECES, wait, 0)


def routes(owner, rank, offs, piece, tiles, rows):
    which = piece % CLASSES
    row = lax.dynamic_index_in_dim(offs, piece // CLASSES, 0, keepdims=False)
    none = tiles * SENT
    before = jnp.where(owner > 0, (owner - 1) * SENT + LOW + rank * SIDE, none)
    after = jnp.where(owner < tiles - 1, (owner + 1) * SENT + HIGH + rank * SIDE, none)
    own = first_of(RAW * jnp.maximum(EDGE - row, 0), which)
    over = first_of(RAW * (EDGE + rows - row), which)
    return jnp.stack([before, owner * SENT + rank * OWN, after, own, over, owner * rows + row - WIN // 2])


def route_kernel(parts, index_ref, in_ref, *refs):
    out_ref, wide_ref, join_ref, narrow_ref, sems = refs[-5:]
    tiles, blocks = in_ref.shape[0], out_ref.shape[0]
    which = lax.axis_index("tiles") & (CLASSES - 1)
    wide_ref[tiles * SENT :, :] = jnp.zeros_like(wide_ref[tiles * SENT :, :])

    def widen(i, carry):
        wide_ref[pl.ds(pl.multiple_of(i * SENT, 16), SENT), :] = in_ref[i].astype(F32)
        return carry

    lax.fori_loop(0, tiles, widen, 0)
    last = jnp.where(which > 0, PROWS - 1, 24)

    def gather(b, carry):
        join_ref[b, 0:8, :] = wide_ref[pl.ds(index_ref[0, b], 8), :]
        join_ref[b, pl.ds(index_ref[3, b], 16), :] = wide_ref[pl.ds(index_ref[1, b], 16), :]
        join_ref[b, pl.ds(index_ref[4, b], 8), :] = wide_ref[pl.ds(index_ref[2, b], 8), :]
        join_ref[b, pl.ds(last, 1), :] = jnp.full((1, 128), index_ref[5, b].astype(F32), F32)
        return carry

    def narrow(b, carry):
        narrow_ref[b] = join_ref[b, 0:PROWS, :].astype(BF16)
        return carry

    each = blocks // parts
    copies = []
    for part in range(parts):
        here = pl.ds(part * each, each)
        lax.fori_loop(part * each, (part + 1) * each, gather, 0, unroll=8)
        lax.fori_loop(part * each, (part + 1) * each, narrow, 0, unroll=8)
        copies.append(pltpu.make_async_copy(narrow_ref.at[here], out_ref.at[here], sems.at[part]))
        copies[-1].start()
    for copy in copies:
        copy.wait()


def nt(a, b):
    return lax.dot_general(a, b, (((1,), (1,)), ((), ())), preferred_element_type=F32)


def rms_scale(values, gain):
    return values * lax.rsqrt(jnp.mean(values * values, axis=-1, keepdims=True) + 1e-06) * gain


def refine_kernel(
    height, raw_ref, wconv_ref, query_ref, wcorr_ref, wfeat_ref, time_ref, start_ref, gain1_ref,
    wk_ref, wq_ref, wv_ref, wout_ref, gain2_ref, wup_ref, wdown_ref, out_ref,
    cells_ref, cols_ref, tok_ref, down_ref, sem,
):
    frames = raw_ref.shape[0] // 128
    step = pl.program_id(0)

    @pl.when(step == 0)
    def _():
        fetch = pltpu.make_async_copy(wdown_ref, down_ref, sem)
        fetch.start()
        for f in range(frames):
            for c in range(CLASSES):
                at = (f * CLASSES + c) * PROWS
                cells_ref[pl.ds(f * 128 + c, PROWS, stride=CLASSES), :] = raw_ref[at : at + PROWS, :].astype(F32)
        cells_ref[frames * 128 :, :] = jnp.zeros_like(cells_ref[frames * 128 :, :])
        line = lax.broadcasted_iota(jnp.int32, (128, 128), 0) // RAW
        line = line.astype(F32)
        feat = jnp.dot(query_ref[...], wfeat_ref[...], preferred_element_type=F32)
        for f in range(frames):
            for a in range(3):
                for b in range(3):
                    at = f * 128 + a * RAW + b
                    cols_ref[f * 128 : (f + 1) * 128, (a * 3 + b) * 128 : (a * 3 + b + 1) * 128] = (
                        cells_ref[at : at + 128, :].astype(BF16)
                    )
        conv = jnp.dot(cols_ref[...], wconv_ref[...], preferred_element_type=F32)
        corr = []
        for f in range(frames):
            info = f * 128 + 127
            row = line + cells_ref[info : info + 1, :]
            inside = (row >= 0) & (row < height)
            here = jnp.where(inside, conv[f * 128 : (f + 1) * 128], 0.0).astype(BF16)
            corr.append((nt(query_ref[...], here) * (128 ** -0.5)).astype(BF16))
        tokens = jnp.dot(
            jnp.concatenate(corr, axis=0), wcorr_ref[...], preferred_element_type=F32
        )
        for f in range(frames):
            here = tokens[f * 128 : (f + 1) * 128] + feat + time_ref[f : f + 1, :]
            for part in range(3):
                tok_ref[part, pl.ds(f, 128, stride=frames), :] = here[
                    :, part * 128 : (part + 1) * 128
                ]
        fetch.wait()

    here = pl.ds(pl.multiple_of(step * CHUNK, CHUNK), CHUNK)
    tokens = jnp.concatenate([tok_ref[part, here, :] for part in range(3)], axis=1)
    normed = rms_scale(tokens, gain1_ref[...]).astype(BF16)
    keys = jnp.dot(normed, wk_ref[...], preferred_element_type=F32).astype(BF16)
    query = nt(wq_ref[...], normed).astype(BF16)
    values = nt(wv_ref[...], normed).astype(BF16)
    track = lax.broadcasted_iota(jnp.int32, (16, 128), 1) // frames
    frame = lax.broadcasted_iota(jnp.int32, (16, 128), 0)
    key_track = lax.broadcasted_iota(jnp.int32, (128, 128), 0) // frames
    query_track = lax.broadcasted_iota(jnp.int32, (128, 128), 1) // frames
    same = (key_track == query_track).astype(BF16)
    factor = HEAD ** -0.5 * 1.4426950408889634
    zeros16 = jnp.zeros((16, 128), BF16)
    zeros64 = jnp.zeros((64, 128), BF16)
    attended = []
    for first in range(0, CHUNK // 128, BATCH):
        some = range(first, first + BATCH)
        own, valid = [], []
        for g in some:
            lanes = slice(g * 128, (g + 1) * 128)
            valid += [frame >= start_ref[0, :, lanes]] * HEADS
            for pair in range(HEADS // 2):
                one = query[2 * pair * HEAD : (2 * pair + 1) * HEAD, lanes]
                two = query[(2 * pair + 1) * HEAD : (2 * pair + 2) * HEAD, lanes]
                both = jnp.concatenate(
                    [
                        jnp.concatenate([one, zeros16, zeros64], axis=0),
                        jnp.concatenate([zeros64, two, zeros16], axis=0),
                    ],
                    axis=1,
                )
                scores = jnp.dot(
                    keys[lanes, pair * 128 : (pair + 1) * 128], both, preferred_element_type=F32
                )
                for h in range(2):
                    full = scores[:, h * 128 : (h + 1) * 128]
                    part = full[0:16, :]
                    for t in range(1, 8):
                        part = jnp.where(track == t, full[16 * t : 16 * (t + 1), :], part)
                    own.append(part)
        own = [jnp.where(v, p, -1e30) for v, p in zip(valid, own)]
        top = [jnp.max(p, axis=0, keepdims=True) for p in own]
        weights = [jnp.exp2((p - t) * factor) for p, t in zip(own, top)]
        total = [jnp.sum(w, axis=0, keepdims=True) for w in weights]
        probs = [(w * (1.0 / t)).astype(BF16) for w, t in zip(weights, total)]
        for g in some:
            lanes = slice(g * 128, (g + 1) * 128)
            heads = []
            for pair in range(HEADS // 2):
                two = [
                    jnp.concatenate([probs[(g - first) * HEADS + 2 * pair + h]] * 8, axis=0) * same
                    for h in range(2)
                ]
                at = 2 * pair * HEAD
                both = jnp.dot(
                    values[at : at + 2 * HEAD, lanes],
                    jnp.concatenate(two, axis=1),
                    preferred_element_type=F32,
                )
                heads += [both[:HEAD, :128], both[HEAD:, 128:]]
            attended.append(jnp.concatenate(heads, axis=0).astype(BF16).T)
    attended = jnp.concatenate(attended, axis=0)
    mixed = tokens + jnp.dot(attended, wout_ref[...], preferred_element_type=F32)
    normed2 = rms_scale(mixed, gain2_ref[...]).astype(BF16)
    hidden = jax.nn.gelu(
        jnp.dot(normed2, wup_ref[...], preferred_element_type=F32), approximate=True
    ).astype(BF16)
    result = mixed + jnp.dot(hidden, down_ref[...], preferred_element_type=F32)
    out_ref[...] = result.astype(BF16)


def params(mib):
    return pltpu.CompilerParams(vmem_limit_bytes=mib << 20)


SMEM = pl.BlockSpec(memory_space=pltpu.SMEM)
VMEM = pl.BlockSpec(memory_space=pltpu.VMEM)
HBM = pl.BlockSpec(memory_space=pltpu.HBM)


def refine_call(height, raw, *rest):
    tokens, dim = rest[5].size, rest[4].shape[1]
    chans = raw.shape[1]
    step = pl.BlockSpec((1, 1, CHUNK), lambda i: (i, 0, 0))
    return pl.pallas_call(
        functools.partial(refine_kernel, height),
        grid=(tokens // CHUNK,),
        out_shape=jax.ShapeDtypeStruct((tokens, dim), BF16),
        in_specs=[VMEM] * 6 + [step] + [VMEM] * (len(rest) - 7) + [HBM],
        out_specs=pl.BlockSpec((CHUNK, dim), lambda i: (i, 0)),
        scratch_shapes=[
            pltpu.VMEM((raw.shape[0] + 32, 128), F32),
            pltpu.VMEM((tokens, 9 * chans), BF16),
            pltpu.VMEM((3, tokens, 128), F32),
            pltpu.VMEM(rest[-1].shape, BF16),
            pltpu.SemaphoreType.DMA,
        ],
        compiler_params=params(32),
        name="refine",
    )(raw, *rest[:-1], pltpu.with_memory_space_constraint(rest[-1], pltpu.HBM))


def body(
    features, w_conv, query_feats, offset_rows, offset_cols, owners, start_frames, w_corr, w_feat,
    time_embed, gain_attn, w_qkv, w_attn_out, gain_mlp, w_up, w_down,
):
    n_tiles = lax.axis_size("tiles")
    frames, rows, width, chans = features.shape
    blocks = owners.shape[0]
    tracks = query_feats.shape[0]
    total = time_embed.shape[0]
    dim = w_feat.shape[1]

    owner = owners[:, 0]
    number = jnp.arange(blocks, dtype=jnp.int32)
    rank = jnp.sum(
        (owner[:, None] == owner[None, :]) & (number[None, :] < number[:, None]), axis=1, dtype=jnp.int32
    )
    hbm = lambda array: pltpu.with_memory_space_constraint(array, pltpu.HBM)
    pieces = pl.pallas_call(
        send_kernel,
        out_shape=pltpu.HBM((PIECES, SENT, chans), BF16),
        in_specs=[HBM] * 4,
        out_specs=HBM,
        scratch_shapes=[
            pltpu.SMEM((blocks,), jnp.int32),
            pltpu.SMEM(offset_cols.shape, jnp.int32),
            pltpu.SMEM(offset_rows.shape, jnp.int32),
            pltpu.VMEM(features.shape, BF16),
            pltpu.SMEM((64,), jnp.int32),
            pltpu.VMEM((TILE, 48, 128), F32),
            pltpu.VMEM((192, 128), F32),
            pltpu.VMEM((PIECES * SENT, 128), F32),
            pltpu.VMEM((PIECES, SENT, chans), BF16),
            pltpu.SemaphoreType.DMA((3,)),
            pltpu.SemaphoreType.DMA((frames,)),
            pltpu.SemaphoreType.DMA((PIECES,)),
        ],
        compiler_params=params(32),
        name="windows",
    )(hbm(owner), hbm(offset_cols), hbm(offset_rows), hbm(features))
    spread = lax.all_to_all(pieces, "tiles", 0, 0, tiled=True)
    wk = jnp.pad(w_qkv[:, dim : 2 * dim].reshape(dim, HEADS, HEAD), ((0, 0), (0, 0), (0, 16)))
    wk = wk.reshape(dim, HEADS * 64)
    wq, wv = w_qkv[:, :dim].T, w_qkv[:, 2 * dim :].T
    wcorr = jnp.pad(w_corr.reshape(WIN, WIN, dim), ((0, 0), (0, RAW - WIN), (0, 0)))
    wcorr = jnp.pad(wcorr.reshape(WIN * RAW, dim), ((0, 128 - WIN * RAW), (0, 0)))
    tokens = tracks * total
    start = jnp.repeat(start_frames, total).reshape(tokens // CHUNK, 1, CHUNK)
    gain1, gain2 = gain_attn.reshape(1, dim), gain_mlp.reshape(1, dim)
    first = (wk, wq, wv, hbm(wcorr), start, gain1, gain2)
    index = routes(owner, rank, offset_rows, lax.axis_index("tiles"), n_tiles, rows)
    routed = pl.pallas_call(
        functools.partial(route_kernel, 4),
        out_shape=jax.ShapeDtypeStruct((blocks, PROWS, chans), BF16),
        in_specs=[SMEM, VMEM] + [HBM] * len(first),
        out_specs=HBM,
        scratch_shapes=[
            pltpu.VMEM((n_tiles * SENT + 16, 128), F32),
            pltpu.VMEM((blocks, 32, 128), F32),
            pltpu.VMEM((blocks, PROWS, chans), BF16),
            pltpu.SemaphoreType.DMA((4,)),
        ],
        compiler_params=params(32),
        name="route",
    )(index, spread, *first)
    raw = lax.all_to_all(routed, ("frames", "tiles"), 0, 0, tiled=True)
    raw = raw.reshape(blocks * PROWS, chans)

    refined = refine_call(
        n_tiles * rows, raw, w_conv.reshape(9 * chans, chans), query_feats, wcorr, w_feat, time_embed,
        start, gain1, wk, wq, wv, w_attn_out, gain2, w_up, w_down,
    )
    return refined.reshape(tracks, total, dim)


def solution(mesh):
    placed = (
        P("frames", "tiles", None, None),
        P(),
        P(("frames", "tiles"), None),
        P("frames", None),
        P("frames", None),
        P(),
        P(("frames", "tiles")),
        P(), P(), P(), P(), P(), P(), P(), P(), P(),
    )
    return jax.shard_map(
        body,
        mesh=mesh,
        in_specs=placed,
        out_specs=P(("frames", "tiles"), None, None),
        check_vma=False,
    )
```

```python
import functools

import jax
import jax.numpy as jnp
from jax import lax
from jax.experimental import pallas as pl
from jax.experimental.pallas import tpu as pltpu
from jax.sharding import PartitionSpec as P

HEADS = 8
HEAD = 48
WIN = 9
RAW = WIN + 2
QBLK = 128
CAP = 12
TILE = 8
EDGE = 5
CLASSES = 8
PIECES = 32
PROWS = 16
OWN = 11
SIDE = 7
LOW = CAP * OWN
HIGH = LOW + CAP * SIDE
SENT = 304
CHUNK = 1024
TOGETHER = 4
BATCH = 4
F32 = jnp.float32
BF16 = jnp.bfloat16


def aligned(col, wide):
    return pl.multiple_of(jnp.clip((col >> 4) << 4, 0, wide - 32), 16)


def first_of(cell, which):
    return (cell - which + CLASSES - 1) >> 3


def send_kernel(
    owners_hbm, cols_hbm, offs_hbm, feat_ref, out_ref, owners_ref, cols_ref, offs_ref, here_ref, ids_ref, tmp_ref,
    flat_ref, piece_ref, narrow_ref, table_sems, sems, out_sems,
):
    frames, rows, wide, _ = feat_ref.shape
    tile = lax.axis_index("tiles")
    tables = [
        pltpu.make_async_copy(source, target, table_sems.at[n])
        for n, (source, target) in enumerate(
            ((owners_hbm, owners_ref), (cols_hbm, cols_ref), (offs_hbm, offs_ref))
        )
    ]
    for copy in tables:
        copy.start()
    copies = [pltpu.make_async_copy(feat_ref.at[k], here_ref.at[k], sems.at[k]) for k in range(frames)]
    for copy in copies:
        copy.start()

    tmp_ref[...] = jnp.zeros_like(tmp_ref)
    flat_ref[...] = jnp.zeros_like(flat_ref)
    for copy in tables:
        copy.wait()

    def scan(b, counts):
        near = owners_ref[b] - tile + 1
        for d in range(3):
            ids_ref[16 * d + counts[d]] = b
        return tuple(counts[d] + (near == d).astype(jnp.int32) for d in range(3))

    zero = jnp.int32(0)
    for n in range(48):
        ids_ref[n] = 0
    counts = lax.fori_loop(0, owners_ref.shape[0], scan, (zero, zero, zero), unroll=8)

    def leave(i):
        return pltpu.make_async_copy(narrow_ref.at[i], out_ref.at[i], out_sems.at[i])

    for k in range(frames):
        copies[k].wait()

        def part(d, row0, count, place, room, k=k):
            def slots(p, carry):
                some = []
                for n in range(TOGETHER):
                    s = p * TOGETHER + n
                    block = ids_ref[16 * d + s]
                    col = cols_ref[k, block] - 1
                    start = aligned(col, wide)
                    tmp_ref[n, 0:count, 8:40, :] = here_ref[k, row0 : row0 + count, pl.ds(start, 32), :].astype(F32)
                    some.append((s, col - start, offs_ref[k, block]))
                for i in range(count):
                    for n, (_, shift, _) in enumerate(some):
                        at = 16 + RAW * i
                        flat_ref[n, at : at + 16, :] = tmp_ref[n, i, pl.ds(8 + shift, 16), :]
                for n, (s, _, row) in enumerate(some):
                    at = RAW * (EDGE - row + row0 + (rows, 0, -rows)[d])
                    low = jnp.maximum(at, 0)
                    for c in range(CLASSES):
                        source = 16 + CLASSES * first_of(low, c) + c - at
                        target = (k * CLASSES + c) * SENT + place + s * room
                        length = 16 if d == 1 else 8
                        piece_ref[pl.ds(target, length), :] = flat_ref[n, pl.ds(source, length, stride=CLASSES), :]
                return carry

            lax.fori_loop(0, (counts[d] + TOGETHER - 1) // TOGETHER, slots, 0)

        part(1, 0, rows, 0, OWN)
        part(2, rows - EDGE, EDGE, LOW, SIDE)
        part(0, 0, EDGE, HIGH, SIDE)

        def narrow(i, carry):
            narrow_ref[i] = piece_ref[pl.ds(pl.multiple_of(i * SENT, 16), SENT), :].astype(BF16)
            leave(i).start()
            return carry

        lax.fori_loop(k * CLASSES, (k + 1) * CLASSES, narrow, 0)

    def wait(i, carry):
        leave(i).wait()
        return carry

    lax.fori_loop(0, PIECES, wait, 0)


def routes(owner, rank, offs, piece, tiles, rows):
    which = piece % CLASSES
    row = lax.dynamic_index_in_dim(offs, piece // CLASSES, 0, keepdims=False)
    none = tiles * SENT
    before = jnp.where(owner > 0, (owner - 1) * SENT + LOW + rank * SIDE, none)
    after = jnp.where(owner < tiles - 1, (owner + 1) * SENT + HIGH + rank * SIDE, none)
    own = first_of(RAW * jnp.maximum(EDGE - row, 0), which)
    over = first_of(RAW * (EDGE + rows - row), which)
    return jnp.stack([before, owner * SENT + rank * OWN, after, own, over, owner * rows + row - WIN // 2])


def route_kernel(index_hbm, in_ref, *refs):
    out_ref, index_ref, wide_ref, join_ref, sem = refs[-5:]
    table = pltpu.make_async_copy(index_hbm, index_ref, sem)
    table.start()
    tiles, blocks = in_ref.shape[0], out_ref.shape[0]
    which = lax.axis_index("tiles") & (CLASSES - 1)
    wide_ref[tiles * SENT :, :] = jnp.zeros_like(wide_ref[tiles * SENT :, :])

    def widen(i, carry):
        wide_ref[pl.ds(pl.multiple_of(i * SENT, 16), SENT), :] = in_ref[i].astype(F32)
        return carry

    lax.fori_loop(0, tiles, widen, 0)
    table.wait()
    last = jnp.where(which > 0, PROWS - 1, 24)

    def gather(b, carry):
        join_ref[b, 0:8, :] = wide_ref[pl.ds(index_ref[0, b], 8), :]
        join_ref[b, pl.ds(index_ref[3, b], 16), :] = wide_ref[pl.ds(index_ref[1, b], 16), :]
        join_ref[b, pl.ds(index_ref[4, b], 8), :] = wide_ref[pl.ds(index_ref[2, b], 8), :]
        join_ref[b, pl.ds(last, 1), :] = jnp.full((1, 128), index_ref[5, b].astype(F32), F32)
        return carry

    def narrow(b, carry):
        out_ref[b] = join_ref[b, 0:PROWS, :].astype(BF16)
        return carry

    lax.fori_loop(0, blocks, gather, 0, unroll=8)
    lax.fori_loop(0, blocks, narrow, 0, unroll=8)


def nt(a, b):
    return lax.dot_general(a, b, (((1,), (1,)), ((), ())), preferred_element_type=F32)


def rms_scale(values, gain):
    return values * lax.rsqrt(jnp.mean(values * values, axis=-1, keepdims=True) + 1e-06) * gain


def refine_kernel(
    height, raw_ref, wconv_ref, query_ref, wcorr_ref, wfeat_ref, time_ref, start_ref, gain1_ref,
    wk_ref, wq_ref, wv_ref, wout_ref, gain2_ref, wup_ref, wdown_ref, out_ref,
    cells_ref, cols_ref, tok_ref, down_ref, sem,
):
    frames = raw_ref.shape[0] // 128
    step = pl.program_id(0)

    @pl.when(step == 0)
    def _():
        fetch = pltpu.make_async_copy(wdown_ref, down_ref, sem)
        fetch.start()
        for f in range(frames):
            for c in range(CLASSES):
                at = (f * CLASSES + c) * PROWS
                cells_ref[pl.ds(f * 128 + c, PROWS, stride=CLASSES), :] = raw_ref[at : at + PROWS, :].astype(F32)
        cells_ref[frames * 128 :, :] = jnp.zeros_like(cells_ref[frames * 128 :, :])
        line = lax.broadcasted_iota(jnp.int32, (128, 128), 0) // RAW
        line = line.astype(F32)
        feat = jnp.dot(query_ref[...], wfeat_ref[...], preferred_element_type=F32)
        for f in range(frames):
            for a in range(3):
                for b in range(3):
                    at = f * 128 + a * RAW + b
                    cols_ref[f * 128 : (f + 1) * 128, (a * 3 + b) * 128 : (a * 3 + b + 1) * 128] = (
                        cells_ref[at : at + 128, :].astype(BF16)
                    )
        conv = jnp.dot(cols_ref[...], wconv_ref[...], preferred_element_type=F32)
        corr = []
        for f in range(frames):
            info = f * 128 + 127
            row = line + cells_ref[info : info + 1, :]
            inside = (row >= 0) & (row < height)
            here = jnp.where(inside, conv[f * 128 : (f + 1) * 128], 0.0).astype(BF16)
            corr.append((nt(query_ref[...], here) * (128 ** -0.5)).astype(BF16))
        tokens = jnp.dot(
            jnp.concatenate(corr, axis=0), wcorr_ref[...], preferred_element_type=F32
        )
        for f in range(frames):
            here = tokens[f * 128 : (f + 1) * 128] + feat + time_ref[f : f + 1, :]
            for part in range(3):
                tok_ref[part, pl.ds(f, 128, stride=frames), :] = here[
                    :, part * 128 : (part + 1) * 128
                ]
        fetch.wait()

    here = pl.ds(pl.multiple_of(step * CHUNK, CHUNK), CHUNK)
    tokens = jnp.concatenate([tok_ref[part, here, :] for part in range(3)], axis=1)
    normed = rms_scale(tokens, gain1_ref[...]).astype(BF16)
    keys = jnp.dot(normed, wk_ref[...], preferred_element_type=F32).astype(BF16)
    query = nt(wq_ref[...], normed).astype(BF16)
    values = nt(wv_ref[...], normed).astype(BF16)
    track = lax.broadcasted_iota(jnp.int32, (16, 128), 1) // frames
    frame = lax.broadcasted_iota(jnp.int32, (16, 128), 0)
    key_track = lax.broadcasted_iota(jnp.int32, (128, 128), 0) // frames
    query_track = lax.broadcasted_iota(jnp.int32, (128, 128), 1) // frames
    same = (key_track == query_track).astype(BF16)
    factor = HEAD ** -0.5 * 1.4426950408889634
    zeros16 = jnp.zeros((16, 128), BF16)
    zeros64 = jnp.zeros((64, 128), BF16)
    attended = []
    for first in range(0, CHUNK // 128, BATCH):
        some = range(first, first + BATCH)
        own, valid = [], []
        for g in some:
            lanes = slice(g * 128, (g + 1) * 128)
            valid += [frame >= start_ref[0, :, lanes]] * HEADS
            for pair in range(HEADS // 2):
                one = query[2 * pair * HEAD : (2 * pair + 1) * HEAD, lanes]
                two = query[(2 * pair + 1) * HEAD : (2 * pair + 2) * HEAD, lanes]
                both = jnp.concatenate(
                    [
                        jnp.concatenate([one, zeros16, zeros64], axis=0),
                        jnp.concatenate([zeros64, two, zeros16], axis=0),
                    ],
                    axis=1,
                )
                scores = jnp.dot(
                    keys[lanes, pair * 128 : (pair + 1) * 128], both, preferred_element_type=F32
                )
                for h in range(2):
                    full = scores[:, h * 128 : (h + 1) * 128]
                    part = full[0:16, :]
                    for t in range(1, 8):
                        part = jnp.where(track == t, full[16 * t : 16 * (t + 1), :], part)
                    own.append(part)
        own = [jnp.where(v, p, -1e30) for v, p in zip(valid, own)]
        top = [jnp.max(p, axis=0, keepdims=True) for p in own]
        weights = [jnp.exp2((p - t) * factor) for p, t in zip(own, top)]
        total = [jnp.sum(w, axis=0, keepdims=True) for w in weights]
        probs = [(w * (1.0 / t)).astype(BF16) for w, t in zip(weights, total)]
        for g in some:
            lanes = slice(g * 128, (g + 1) * 128)
            heads = []
            for pair in range(HEADS // 2):
                two = [
                    jnp.concatenate([probs[(g - first) * HEADS + 2 * pair + h]] * 8, axis=0) * same
                    for h in range(2)
                ]
                at = 2 * pair * HEAD
                both = jnp.dot(
                    values[at : at + 2 * HEAD, lanes],
                    jnp.concatenate(two, axis=1),
                    preferred_element_type=F32,
                )
                heads += [both[:HEAD, :128], both[HEAD:, 128:]]
            attended.append(jnp.concatenate(heads, axis=0).astype(BF16).T)
    attended = jnp.concatenate(attended, axis=0)
    mixed = tokens + jnp.dot(attended, wout_ref[...], preferred_element_type=F32)
    normed2 = rms_scale(mixed, gain2_ref[...]).astype(BF16)
    hidden = jax.nn.gelu(
        jnp.dot(normed2, wup_ref[...], preferred_element_type=F32), approximate=True
    ).astype(BF16)
    result = mixed + jnp.dot(hidden, down_ref[...], preferred_element_type=F32)
    out_ref[...] = result.astype(BF16)


def params(mib):
    return pltpu.CompilerParams(vmem_limit_bytes=mib << 20)


SMEM = pl.BlockSpec(memory_space=pltpu.SMEM)
VMEM = pl.BlockSpec(memory_space=pltpu.VMEM)
HBM = pl.BlockSpec(memory_space=pltpu.HBM)


def refine_call(height, raw, *rest):
    tokens, dim = rest[5].size, rest[4].shape[1]
    chans = raw.shape[1]
    step = pl.BlockSpec((1, 1, CHUNK), lambda i: (i, 0, 0))
    return pl.pallas_call(
        functools.partial(refine_kernel, height),
        grid=(tokens // CHUNK,),
        out_shape=jax.ShapeDtypeStruct((tokens, dim), BF16),
        in_specs=[VMEM] * 6 + [step] + [VMEM] * (len(rest) - 7) + [HBM],
        out_specs=pl.BlockSpec((CHUNK, dim), lambda i: (i, 0)),
        scratch_shapes=[
            pltpu.VMEM((raw.shape[0] + 32, 128), F32),
            pltpu.VMEM((tokens, 9 * chans), BF16),
            pltpu.VMEM((3, tokens, 128), F32),
            pltpu.VMEM(rest[-1].shape, BF16),
            pltpu.SemaphoreType.DMA,
        ],
        compiler_params=params(32),
        name="refine",
    )(raw, *rest[:-1], pltpu.with_memory_space_constraint(rest[-1], pltpu.HBM))


def body(
    features, w_conv, query_feats, offset_rows, offset_cols, owners, start_frames, w_corr, w_feat,
    time_embed, gain_attn, w_qkv, w_attn_out, gain_mlp, w_up, w_down,
):
    n_tiles = lax.axis_size("tiles")
    frames, rows, width, chans = features.shape
    blocks = owners.shape[0]
    tracks = query_feats.shape[0]
    total = time_embed.shape[0]
    dim = w_feat.shape[1]

    owner = owners[:, 0]
    number = jnp.arange(blocks, dtype=jnp.int32)
    rank = jnp.sum(
        (owner[:, None] == owner[None, :]) & (number[None, :] < number[:, None]), axis=1, dtype=jnp.int32
    )
    hbm = lambda array: pltpu.with_memory_space_constraint(array, pltpu.HBM)
    pieces = pl.pallas_call(
        send_kernel,
        out_shape=pltpu.HBM((PIECES, SENT, chans), BF16),
        in_specs=[HBM] * 4,
        out_specs=HBM,
        scratch_shapes=[
            pltpu.SMEM((blocks,), jnp.int32),
            pltpu.SMEM(offset_cols.shape, jnp.int32),
            pltpu.SMEM(offset_rows.shape, jnp.int32),
            pltpu.VMEM(features.shape, BF16),
            pltpu.SMEM((64,), jnp.int32),
            pltpu.VMEM((TOGETHER, TILE, 48, 128), F32),
            pltpu.VMEM((TOGETHER, 192, 128), F32),
            pltpu.VMEM((PIECES * SENT, 128), F32),
            pltpu.VMEM((PIECES, SENT, chans), BF16),
            pltpu.SemaphoreType.DMA((3,)),
            pltpu.SemaphoreType.DMA((frames,)),
            pltpu.SemaphoreType.DMA((PIECES,)),
        ],
        compiler_params=params(32),
        name="windows",
    )(hbm(owner), hbm(offset_cols), hbm(offset_rows), hbm(features))
    spread = lax.all_to_all(pieces, "tiles", 0, 0, tiled=True)
    wk = jnp.pad(w_qkv[:, dim : 2 * dim].reshape(dim, HEADS, HEAD), ((0, 0), (0, 0), (0, 16)))
    wk = wk.reshape(dim, HEADS * 64)
    wq, wv = w_qkv[:, :dim].T, w_qkv[:, 2 * dim :].T
    wcorr = jnp.pad(w_corr.reshape(WIN, WIN, dim), ((0, 0), (0, RAW - WIN), (0, 0)))
    wcorr = jnp.pad(wcorr.reshape(WIN * RAW, dim), ((0, 128 - WIN * RAW), (0, 0)))
    tokens = tracks * total
    start = jnp.repeat(start_frames, total).reshape(tokens // CHUNK, 1, CHUNK)
    gain1, gain2 = gain_attn.reshape(1, dim), gain_mlp.reshape(1, dim)
    first = (wk, wq, wv, hbm(wcorr), start, gain1, gain2)
    index = routes(owner, rank, offset_rows, lax.axis_index("tiles"), n_tiles, rows)
    routed = pl.pallas_call(
        route_kernel,
        out_shape=jax.ShapeDtypeStruct((blocks, PROWS, chans), BF16),
        in_specs=[HBM, VMEM] + [HBM] * len(first),
        out_specs=VMEM,
        scratch_shapes=[
            pltpu.SMEM(index.shape, jnp.int32),
            pltpu.VMEM((n_tiles * SENT + 16, 128), F32),
            pltpu.VMEM((blocks, 32, 128), F32),
            pltpu.SemaphoreType.DMA,
        ],
        compiler_params=params(32),
        name="route",
    )(index, spread, *first)
    raw = lax.all_to_all(routed, ("frames", "tiles"), 0, 0, tiled=True)
    raw = raw.reshape(blocks * PROWS, chans)

    refined = refine_call(
        n_tiles * rows, raw, w_conv.reshape(9 * chans, chans), query_feats, wcorr, w_feat, time_embed,
        start, gain1, wk, wq, wv, w_attn_out, gain2, w_up, w_down,
    )
    return refined.reshape(tracks, total, dim)


def solution(mesh):
    placed = (
        P("frames", "tiles", None, None),
        P(),
        P(("frames", "tiles"), None),
        P("frames", None),
        P("frames", None),
        P(),
        P(("frames", "tiles")),
        P(), P(), P(), P(), P(), P(), P(), P(), P(),
    )
    return jax.shard_map(
        body,
        mesh=mesh,
        in_specs=placed,
        out_specs=P(("frames", "tiles"), None, None),
        check_vma=False,
    )
```

```python
import functools

import jax
import jax.numpy as jnp
from jax import lax
from jax.experimental import pallas as pl
from jax.experimental.pallas import tpu as pltpu
from jax.sharding import PartitionSpec as P

HEADS = 8
HEAD = 48
WIN = 9
RAW = WIN + 2
QBLK = 128
CAP = 12
TILE = 8
EDGE = 5
CLASSES = 8
PIECES = 32
PROWS = 16
OWN = 11
SIDE = 7
LOW = CAP * OWN
HIGH = LOW + CAP * SIDE
SENT = 304
CHUNK = 1024
TOGETHER = 4
BATCH = 4
F32 = jnp.float32
BF16 = jnp.bfloat16


def aligned(col, wide):
    return pl.multiple_of(jnp.clip((col >> 4) << 4, 0, wide - 32), 16)


def first_of(cell, which):
    return (cell - which + CLASSES - 1) >> 3


def send_kernel(
    owners_hbm, cols_hbm, offs_hbm, feat_ref, out_ref, owners_ref, cols_ref, offs_ref, here_ref, ids_ref, tmp_ref,
    flat_ref, piece_ref, narrow_ref, table_sems, sems, out_sems,
):
    frames, rows, wide, _ = feat_ref.shape
    tile = lax.axis_index("tiles")
    tables = [
        pltpu.make_async_copy(source, target, table_sems.at[n])
        for n, (source, target) in enumerate(
            ((owners_hbm, owners_ref), (cols_hbm, cols_ref), (offs_hbm, offs_ref))
        )
    ]
    for copy in tables:
        copy.start()
    copies = [pltpu.make_async_copy(feat_ref.at[k], here_ref.at[k], sems.at[k]) for k in range(frames)]
    for copy in copies:
        copy.start()

    tmp_ref[...] = jnp.zeros_like(tmp_ref)
    flat_ref[...] = jnp.zeros_like(flat_ref)
    for copy in tables:
        copy.wait()

    def scan(b, counts):
        near = owners_ref[b] - tile + 1
        for d in range(3):
            ids_ref[16 * d + counts[d]] = b
        return tuple(counts[d] + (near == d).astype(jnp.int32) for d in range(3))

    zero = jnp.int32(0)
    for n in range(48):
        ids_ref[n] = 0
    counts = lax.fori_loop(0, owners_ref.shape[0], scan, (zero, zero, zero), unroll=8)

    def leave(i):
        return pltpu.make_async_copy(narrow_ref.at[i], out_ref.at[i], out_sems.at[i])

    for k in range(frames):
        copies[k].wait()

        def part(d, row0, count, place, room, k=k):
            def slots(p, carry):
                some = []
                for n in range(TOGETHER):
                    s = p * TOGETHER + n
                    block = ids_ref[16 * d + s]
                    col = cols_ref[k, block] - 1
                    start = aligned(col, wide)
                    tmp_ref[n, 0:count, 8:40, :] = here_ref[k, row0 : row0 + count, pl.ds(start, 32), :].astype(F32)
                    some.append((s, col - start, offs_ref[k, block]))
                for i in range(count):
                    for n, (_, shift, _) in enumerate(some):
                        at = 16 + RAW * i
                        flat_ref[n, at : at + 16, :] = tmp_ref[n, i, pl.ds(8 + shift, 16), :]
                for n, (s, _, row) in enumerate(some):
                    at = RAW * (EDGE - row + row0 + (rows, 0, -rows)[d])
                    low = jnp.maximum(at, 0)
                    for c in range(CLASSES):
                        source = 16 + CLASSES * first_of(low, c) + c - at
                        target = (k * CLASSES + c) * SENT + place + s * room
                        length = 16 if d == 1 else 8
                        piece_ref[pl.ds(target, length), :] = flat_ref[n, pl.ds(source, length, stride=CLASSES), :]
                return carry

            lax.fori_loop(0, (counts[d] + TOGETHER - 1) // TOGETHER, slots, 0)

        part(1, 0, rows, 0, OWN)
        part(2, rows - EDGE, EDGE, LOW, SIDE)
        part(0, 0, EDGE, HIGH, SIDE)

        def narrow(i, carry):
            narrow_ref[i] = piece_ref[pl.ds(pl.multiple_of(i * SENT, 16), SENT), :].astype(BF16)
            leave(i).start()
            return carry

        lax.fori_loop(k * CLASSES, (k + 1) * CLASSES, narrow, 0, unroll=4)

    def wait(i, carry):
        leave(i).wait()
        return carry

    lax.fori_loop(0, PIECES, wait, 0)


def routes(owner, rank, offs, piece, tiles, rows):
    which = piece % CLASSES
    row = lax.dynamic_index_in_dim(offs, piece // CLASSES, 0, keepdims=False)
    none = tiles * SENT
    before = jnp.where(owner > 0, (owner - 1) * SENT + LOW + rank * SIDE, none)
    after = jnp.where(owner < tiles - 1, (owner + 1) * SENT + HIGH + rank * SIDE, none)
    own = first_of(RAW * jnp.maximum(EDGE - row, 0), which)
    over = first_of(RAW * (EDGE + rows - row), which)
    return jnp.stack([before, owner * SENT + rank * OWN, after, own, over, owner * rows + row - WIN // 2])


def route_kernel(index_hbm, in_ref, *refs):
    out_ref, index_ref, wide_ref, join_ref, sem = refs[-5:]
    table = pltpu.make_async_copy(index_hbm, index_ref, sem)
    table.start()
    tiles, blocks = in_ref.shape[0], out_ref.shape[0]
    which = lax.axis_index("tiles") & (CLASSES - 1)
    wide_ref[tiles * SENT :, :] = jnp.zeros_like(wide_ref[tiles * SENT :, :])

    def widen(i, carry):
        wide_ref[pl.ds(pl.multiple_of(i * SENT, 16), SENT), :] = in_ref[i].astype(F32)
        return carry

    lax.fori_loop(0, tiles, widen, 0)
    table.wait()
    last = jnp.where(which > 0, PROWS - 1, 24)

    def gather(b, carry):
        join_ref[b, 0:8, :] = wide_ref[pl.ds(index_ref[0, b], 8), :]
        join_ref[b, pl.ds(index_ref[3, b], 16), :] = wide_ref[pl.ds(index_ref[1, b], 16), :]
        join_ref[b, pl.ds(index_ref[4, b], 8), :] = wide_ref[pl.ds(index_ref[2, b], 8), :]
        join_ref[b, pl.ds(last, 1), :] = jnp.full((1, 128), index_ref[5, b].astype(F32), F32)
        return carry

    def narrow(b, carry):
        out_ref[b] = join_ref[b, 0:PROWS, :].astype(BF16)
        return carry

    lax.fori_loop(0, blocks, gather, 0, unroll=8)
    lax.fori_loop(0, blocks, narrow, 0, unroll=8)


def nt(a, b):
    return lax.dot_general(a, b, (((1,), (1,)), ((), ())), preferred_element_type=F32)


def rms_scale(values, gain):
    return values * lax.rsqrt(jnp.mean(values * values, axis=-1, keepdims=True) + 1e-06) * gain


def refine_kernel(
    height, raw_ref, wconv_ref, query_ref, wcorr_ref, wfeat_ref, time_ref, start_ref, gain1_ref,
    wk_ref, wqv_ref, wout_ref, gain2_ref, wup_ref, wdown_ref, out_ref,
    cells_ref, cols_ref, tok_ref, down_ref, sem,
):
    frames = raw_ref.shape[0] // 128
    step = pl.program_id(0)

    @pl.when(step == 0)
    def _():
        fetch = pltpu.make_async_copy(wdown_ref, down_ref, sem)
        fetch.start()
        for f in range(frames):
            for c in range(CLASSES):
                at = (f * CLASSES + c) * PROWS
                cells_ref[pl.ds(f * 128 + c, PROWS, stride=CLASSES), :] = raw_ref[at : at + PROWS, :].astype(F32)
        cells_ref[frames * 128 :, :] = jnp.zeros_like(cells_ref[frames * 128 :, :])
        line = lax.broadcasted_iota(jnp.int32, (112, 128), 0) // RAW
        line = line.astype(F32)
        feat = jnp.dot(query_ref[...], wfeat_ref[...], preferred_element_type=F32)
        for f in range(frames):
            for a in range(3):
                for b in range(3):
                    at = f * 128 + a * RAW + b
                    cols_ref[f * 112 : (f + 1) * 112, (a * 3 + b) * 128 : (a * 3 + b + 1) * 128] = (
                        cells_ref[at : at + 112, :].astype(BF16)
                    )
        conv = jnp.dot(cols_ref[...], wconv_ref[...], preferred_element_type=F32)
        corr = []
        for f in range(frames):
            info = f * 128 + 127
            row = line + cells_ref[info : info + 1, :]
            inside = (row >= 0) & (row < height)
            here = jnp.where(inside, conv[f * 112 : (f + 1) * 112], 0.0).astype(BF16)
            corr.append((nt(query_ref[...], here) * (128 ** -0.5)).astype(BF16))
        tokens = jnp.dot(
            jnp.concatenate(corr, axis=0), wcorr_ref[...], preferred_element_type=F32
        )
        for f in range(frames):
            here = tokens[f * 128 : (f + 1) * 128] + feat + time_ref[f : f + 1, :]
            for part in range(3):
                tok_ref[part, pl.ds(f, 128, stride=frames), :] = here[
                    :, part * 128 : (part + 1) * 128
                ]
        fetch.wait()

    here = pl.ds(pl.multiple_of(step * CHUNK, CHUNK), CHUNK)
    tokens = jnp.concatenate([tok_ref[part, here, :] for part in range(3)], axis=1)
    normed = rms_scale(tokens, gain1_ref[...]).astype(BF16)
    keys = jnp.dot(normed, wk_ref[...], preferred_element_type=F32).astype(BF16)
    both = nt(wqv_ref[...], normed).astype(BF16)
    query, values = both[: HEADS * HEAD], both[HEADS * HEAD :]
    track = lax.broadcasted_iota(jnp.int32, (16, 128), 1) // frames
    frame = lax.broadcasted_iota(jnp.int32, (16, 128), 0)
    key_track = lax.broadcasted_iota(jnp.int32, (128, 128), 0) // frames
    query_track = lax.broadcasted_iota(jnp.int32, (128, 128), 1) // frames
    same = (key_track == query_track).astype(BF16)
    factor = HEAD ** -0.5 * 1.4426950408889634
    zeros16 = jnp.zeros((16, 128), BF16)
    zeros64 = jnp.zeros((64, 128), BF16)
    attended = []
    for first in range(0, CHUNK // 128, BATCH):
        some = range(first, first + BATCH)
        own, valid = [], []
        for g in some:
            lanes = slice(g * 128, (g + 1) * 128)
            valid += [frame >= start_ref[0, :, lanes]] * HEADS
            for pair in range(HEADS // 2):
                one = query[2 * pair * HEAD : (2 * pair + 1) * HEAD, lanes]
                two = query[(2 * pair + 1) * HEAD : (2 * pair + 2) * HEAD, lanes]
                both = jnp.concatenate(
                    [
                        jnp.concatenate([one, zeros16, zeros64], axis=0),
                        jnp.concatenate([zeros64, two, zeros16], axis=0),
                    ],
                    axis=1,
                )
                scores = jnp.dot(
                    keys[lanes, pair * 128 : (pair + 1) * 128], both, preferred_element_type=F32
                )
                for h in range(2):
                    full = scores[:, h * 128 : (h + 1) * 128]
                    part = full[0:16, :]
                    for t in range(1, 8):
                        part = jnp.where(track == t, full[16 * t : 16 * (t + 1), :], part)
                    own.append(part)
        own = [jnp.where(v, p, -1e30) for v, p in zip(valid, own)]
        top = [jnp.max(p, axis=0, keepdims=True) for p in own]
        weights = [jnp.exp2((p - t) * factor) for p, t in zip(own, top)]
        total = [jnp.sum(w, axis=0, keepdims=True) for w in weights]
        probs = [(w * (1.0 / t)).astype(BF16) for w, t in zip(weights, total)]
        for g in some:
            lanes = slice(g * 128, (g + 1) * 128)
            heads = []
            for pair in range(HEADS // 2):
                two = [
                    jnp.concatenate([probs[(g - first) * HEADS + 2 * pair + h]] * 8, axis=0) * same
                    for h in range(2)
                ]
                at = 2 * pair * HEAD
                both = jnp.dot(
                    values[at : at + 2 * HEAD, lanes],
                    jnp.concatenate(two, axis=1),
                    preferred_element_type=F32,
                )
                heads += [both[:HEAD, :128], both[HEAD:, 128:]]
            attended.append(jnp.concatenate(heads, axis=0).astype(BF16).T)
    attended = jnp.concatenate(attended, axis=0)
    mixed = tokens + jnp.dot(attended, wout_ref[...], preferred_element_type=F32)
    normed2 = rms_scale(mixed, gain2_ref[...]).astype(BF16)
    hidden = jax.nn.gelu(
        jnp.dot(normed2, wup_ref[...], preferred_element_type=F32), approximate=True
    ).astype(BF16)
    result = mixed + jnp.dot(hidden, down_ref[...], preferred_element_type=F32)
    out_ref[...] = result.astype(BF16)


def params(mib):
    return pltpu.CompilerParams(vmem_limit_bytes=mib << 20)


SMEM = pl.BlockSpec(memory_space=pltpu.SMEM)
VMEM = pl.BlockSpec(memory_space=pltpu.VMEM)
HBM = pl.BlockSpec(memory_space=pltpu.HBM)


def refine_call(height, raw, *rest):
    tokens, dim = rest[5].size, rest[4].shape[1]
    chans = raw.shape[1]
    step = pl.BlockSpec((1, 1, CHUNK), lambda i: (i, 0, 0))
    return pl.pallas_call(
        functools.partial(refine_kernel, height),
        grid=(tokens // CHUNK,),
        out_shape=jax.ShapeDtypeStruct((tokens, dim), BF16),
        in_specs=[VMEM] * 6 + [step] + [VMEM] * (len(rest) - 7) + [HBM],
        out_specs=pl.BlockSpec((CHUNK, dim), lambda i: (i, 0)),
        scratch_shapes=[
            pltpu.VMEM((raw.shape[0] + 32, 128), F32),
            pltpu.VMEM((tokens // 128 * 112, 9 * chans), BF16),
            pltpu.VMEM((3, tokens, 128), F32),
            pltpu.VMEM(rest[-1].shape, BF16),
            pltpu.SemaphoreType.DMA,
        ],
        compiler_params=params(32),
        name="refine",
    )(raw, *rest[:-1], pltpu.with_memory_space_constraint(rest[-1], pltpu.HBM))


def body(
    features, w_conv, query_feats, offset_rows, offset_cols, owners, start_frames, w_corr, w_feat,
    time_embed, gain_attn, w_qkv, w_attn_out, gain_mlp, w_up, w_down,
):
    n_tiles = lax.axis_size("tiles")
    frames, rows, width, chans = features.shape
    blocks = owners.shape[0]
    tracks = query_feats.shape[0]
    total = time_embed.shape[0]
    dim = w_feat.shape[1]

    owner = owners[:, 0]
    number = jnp.arange(blocks, dtype=jnp.int32)
    rank = jnp.sum(
        (owner[:, None] == owner[None, :]) & (number[None, :] < number[:, None]), axis=1, dtype=jnp.int32
    )
    hbm = lambda array: pltpu.with_memory_space_constraint(array, pltpu.HBM)
    pieces = pl.pallas_call(
        send_kernel,
        out_shape=pltpu.HBM((PIECES, SENT, chans), BF16),
        in_specs=[HBM] * 4,
        out_specs=HBM,
        scratch_shapes=[
            pltpu.SMEM((blocks,), jnp.int32),
            pltpu.SMEM(offset_cols.shape, jnp.int32),
            pltpu.SMEM(offset_rows.shape, jnp.int32),
            pltpu.VMEM(features.shape, BF16),
            pltpu.SMEM((64,), jnp.int32),
            pltpu.VMEM((TOGETHER, TILE, 48, 128), F32),
            pltpu.VMEM((TOGETHER, 192, 128), F32),
            pltpu.VMEM((PIECES * SENT, 128), F32),
            pltpu.VMEM((PIECES, SENT, chans), BF16),
            pltpu.SemaphoreType.DMA((3,)),
            pltpu.SemaphoreType.DMA((frames,)),
            pltpu.SemaphoreType.DMA((PIECES,)),
        ],
        compiler_params=params(32),
        name="windows",
    )(hbm(owner), hbm(offset_cols), hbm(offset_rows), hbm(features))
    spread = lax.all_to_all(pieces, "tiles", 0, 0, tiled=True)
    wk = jnp.pad(w_qkv[:, dim : 2 * dim].reshape(dim, HEADS, HEAD), ((0, 0), (0, 0), (0, 16)))
    wk = wk.reshape(dim, HEADS * 64)
    wqv = jnp.concatenate([w_qkv[:, :dim], w_qkv[:, 2 * dim :]], axis=1).T
    wcorr = jnp.pad(w_corr.reshape(WIN, WIN, dim), ((0, 0), (0, RAW - WIN), (0, 0)))
    wcorr = jnp.pad(wcorr.reshape(WIN * RAW, dim), ((0, 112 - WIN * RAW), (0, 0)))
    tokens = tracks * total
    start = jnp.repeat(start_frames, total).reshape(tokens // CHUNK, 1, CHUNK)
    gain1, gain2 = gain_attn.reshape(1, dim), gain_mlp.reshape(1, dim)
    first = (wk, wqv, hbm(wcorr), start, gain1, gain2)
    index = routes(owner, rank, offset_rows, lax.axis_index("tiles"), n_tiles, rows)
    routed = pl.pallas_call(
        route_kernel,
        out_shape=jax.ShapeDtypeStruct((blocks, PROWS, chans), BF16),
        in_specs=[HBM, VMEM] + [HBM] * len(first),
        out_specs=VMEM,
        scratch_shapes=[
            pltpu.SMEM(index.shape, jnp.int32),
            pltpu.VMEM((n_tiles * SENT + 16, 128), F32),
            pltpu.VMEM((blocks, 32, 128), F32),
            pltpu.SemaphoreType.DMA,
        ],
        compiler_params=params(32),
        name="route",
    )(index, spread, *first)
    raw = lax.all_to_all(routed, ("frames", "tiles"), 0, 0, tiled=True)
    raw = raw.reshape(blocks * PROWS, chans)

    refined = refine_call(
        n_tiles * rows, raw, w_conv.reshape(9 * chans, chans), query_feats, wcorr, w_feat, time_embed,
        start, gain1, wk, wqv, w_attn_out, gain2, w_up, w_down,
    )
    return refined.reshape(tracks, total, dim)


def solution(mesh):
    placed = (
        P("frames", "tiles", None, None),
        P(),
        P(("frames", "tiles"), None),
        P("frames", None),
        P("frames", None),
        P(),
        P(("frames", "tiles")),
        P(), P(), P(), P(), P(), P(), P(), P(), P(),
    )
    return jax.shard_map(
        body,
        mesh=mesh,
        in_specs=placed,
        out_specs=P(("frames", "tiles"), None, None),
        check_vma=False,
    )
```

```python
import functools

import jax
import jax.numpy as jnp
from jax import lax
from jax.experimental import pallas as pl
from jax.experimental.pallas import tpu as pltpu
from jax.sharding import PartitionSpec as P

HEADS = 8
HEAD = 48
WIN = 9
RAW = WIN + 2
QBLK = 128
CAP = 12
TILE = 8
EDGE = 5
CLASSES = 8
PIECES = 32
PROWS = 16
OWN = 11
SIDE = 7
LOW = CAP * OWN
HIGH = LOW + CAP * SIDE
SENT = 304
CHUNK = 1024
TOGETHER = 4
BATCH = 4
F32 = jnp.float32
BF16 = jnp.bfloat16


def aligned(col, wide):
    return pl.multiple_of(jnp.clip((col >> 4) << 4, 0, wide - 32), 16)


def first_of(cell, which):
    return (cell - which + CLASSES - 1) >> 3


def send_kernel(
    owners_hbm, cols_hbm, offs_hbm, feat_ref, out_ref, owners_ref, cols_ref, offs_ref, here_ref, ids_ref, tmp_ref,
    flat_ref, piece_ref, narrow_ref, table_sems, sems, out_sems,
):
    frames, rows, wide, _ = feat_ref.shape
    tile = lax.axis_index("tiles")
    tables = [
        pltpu.make_async_copy(source, target, table_sems.at[n])
        for n, (source, target) in enumerate(
            ((owners_hbm, owners_ref), (cols_hbm, cols_ref), (offs_hbm, offs_ref))
        )
    ]
    for copy in tables:
        copy.start()
    copies = [pltpu.make_async_copy(feat_ref.at[k], here_ref.at[k], sems.at[k]) for k in range(frames)]
    for copy in copies:
        copy.start()

    tmp_ref[...] = jnp.zeros_like(tmp_ref)
    flat_ref[...] = jnp.zeros_like(flat_ref)
    for copy in tables:
        copy.wait()

    def scan(b, counts):
        near = owners_ref[b] - tile + 1
        for d in range(3):
            ids_ref[16 * d + counts[d]] = b
        return tuple(counts[d] + (near == d).astype(jnp.int32) for d in range(3))

    zero = jnp.int32(0)
    for n in range(48):
        ids_ref[n] = 0
    counts = lax.fori_loop(0, owners_ref.shape[0], scan, (zero, zero, zero), unroll=8)

    def leave(i):
        return pltpu.make_async_copy(narrow_ref.at[i], out_ref.at[i], out_sems.at[i])

    for k in range(frames):
        copies[k].wait()

        def part(d, row0, count, place, room, k=k):
            def slots(p, carry):
                some = []
                for n in range(TOGETHER):
                    s = p * TOGETHER + n
                    block = ids_ref[16 * d + s]
                    col = cols_ref[k, block] - 1
                    start = aligned(col, wide)
                    tmp_ref[n, 0:count, 8:40, :] = here_ref[k, row0 : row0 + count, pl.ds(start, 32), :].astype(F32)
                    some.append((s, col - start, offs_ref[k, block]))
                for i in range(count):
                    for n, (_, shift, _) in enumerate(some):
                        at = 16 + RAW * i
                        flat_ref[n, at : at + 16, :] = tmp_ref[n, i, pl.ds(8 + shift, 16), :]
                for n, (s, _, row) in enumerate(some):
                    at = RAW * (EDGE - row + row0 + (rows, 0, -rows)[d])
                    low = jnp.maximum(at, 0)
                    for c in range(CLASSES):
                        source = 16 + CLASSES * first_of(low, c) + c - at
                        target = (k * CLASSES + c) * SENT + place + s * room
                        length = 16 if d == 1 else 8
                        piece_ref[pl.ds(target, length), :] = flat_ref[n, pl.ds(source, length, stride=CLASSES), :]
                return carry

            lax.fori_loop(0, (counts[d] + TOGETHER - 1) // TOGETHER, slots, 0)

        part(1, 0, rows, 0, OWN)
        part(2, rows - EDGE, EDGE, LOW, SIDE)
        part(0, 0, EDGE, HIGH, SIDE)

        def narrow(i, carry):
            narrow_ref[i] = piece_ref[pl.ds(pl.multiple_of(i * SENT, 16), SENT), :].astype(BF16)
            leave(i).start()
            return carry

        lax.fori_loop(k * CLASSES, (k + 1) * CLASSES, narrow, 0, unroll=4)

    def wait(i, carry):
        leave(i).wait()
        return carry

    lax.fori_loop(0, PIECES, wait, 0)


def routes(owner, rank, offs, piece, tiles, rows):
    which = piece % CLASSES
    row = lax.dynamic_index_in_dim(offs, piece // CLASSES, 0, keepdims=False)
    none = tiles * SENT
    turned = tiles - 1 - owner
    before = jnp.where(owner > 0, (turned + 1) * SENT + LOW + rank * SIDE, none)
    after = jnp.where(owner < tiles - 1, (turned - 1) * SENT + HIGH + rank * SIDE, none)
    own = first_of(RAW * jnp.maximum(EDGE - row, 0), which)
    over = first_of(RAW * (EDGE + rows - row), which)
    return jnp.stack([before, turned * SENT + rank * OWN, after, own, over, owner * rows + row - WIN // 2])


def route_kernel(index_hbm, in_ref, *refs):
    out_ref, index_ref, wide_ref, join_ref, sem = refs[-5:]
    table = pltpu.make_async_copy(index_hbm, index_ref, sem)
    table.start()
    tiles, blocks = in_ref.shape[0], out_ref.shape[0]
    which = (tiles - 1 - lax.axis_index("tiles")) & (CLASSES - 1)
    wide_ref[tiles * SENT :, :] = jnp.zeros_like(wide_ref[tiles * SENT :, :])

    def widen(i, carry):
        wide_ref[pl.ds(pl.multiple_of(i * SENT, 16), SENT), :] = in_ref[i].astype(F32)
        return carry

    lax.fori_loop(0, tiles, widen, 0)
    table.wait()
    last = jnp.where(which > 0, PROWS - 1, 24)

    def gather(b, carry):
        join_ref[b, 0:8, :] = wide_ref[pl.ds(index_ref[0, b], 8), :]
        join_ref[b, pl.ds(index_ref[3, b], 16), :] = wide_ref[pl.ds(index_ref[1, b], 16), :]
        join_ref[b, pl.ds(index_ref[4, b], 8), :] = wide_ref[pl.ds(index_ref[2, b], 8), :]
        join_ref[b, pl.ds(last, 1), :] = jnp.full((1, 128), index_ref[5, b].astype(F32), F32)
        return carry

    def narrow(b, carry):
        out_ref[b] = join_ref[b, 0:PROWS, :].astype(BF16)
        return carry

    lax.fori_loop(0, blocks, gather, 0, unroll=8)
    lax.fori_loop(0, blocks, narrow, 0, unroll=8)


def nt(a, b):
    return lax.dot_general(a, b, (((1,), (1,)), ((), ())), preferred_element_type=F32)


def rms_scale(values, gain):
    return values * lax.rsqrt(jnp.mean(values * values, axis=-1, keepdims=True) + 1e-06) * gain


def refine_kernel(
    height, raw_ref, wconv_ref, query_ref, wcorr_ref, wfeat_ref, time_ref, start_ref, gain1_ref,
    wk_ref, wqv_ref, wout_ref, gain2_ref, wup_ref, wdown_ref, out_ref,
    cells_ref, cols_ref, tok_ref, down_ref, sem,
):
    frames = raw_ref.shape[0] // 128
    step = pl.program_id(0)

    @pl.when(step == 0)
    def _():
        fetch = pltpu.make_async_copy(wdown_ref, down_ref, sem)
        fetch.start()
        for f in range(frames):
            for c in range(CLASSES):
                group, k = divmod(f, PIECES // CLASSES)
                at = (group * PIECES + PIECES - 1 - k * CLASSES - c) * PROWS
                cells_ref[pl.ds(f * 128 + c, PROWS, stride=CLASSES), :] = raw_ref[at : at + PROWS, :].astype(F32)
        cells_ref[frames * 128 :, :] = jnp.zeros_like(cells_ref[frames * 128 :, :])
        line = lax.broadcasted_iota(jnp.int32, (112, 128), 0) // RAW
        line = line.astype(F32)
        feat = jnp.dot(query_ref[...], wfeat_ref[...], preferred_element_type=F32)
        for f in range(frames):
            for a in range(3):
                for b in range(3):
                    at = f * 128 + a * RAW + b
                    cols_ref[f * 112 : (f + 1) * 112, (a * 3 + b) * 128 : (a * 3 + b + 1) * 128] = (
                        cells_ref[at : at + 112, :].astype(BF16)
                    )
        conv = jnp.dot(cols_ref[...], wconv_ref[...], preferred_element_type=F32)
        corr = []
        for f in range(frames):
            info = f * 128 + 127
            row = line + cells_ref[info : info + 1, :]
            inside = (row >= 0) & (row < height)
            here = jnp.where(inside, conv[f * 112 : (f + 1) * 112], 0.0).astype(BF16)
            corr.append((nt(query_ref[...], here) * (128 ** -0.5)).astype(BF16))
        tokens = jnp.dot(
            jnp.concatenate(corr, axis=0), wcorr_ref[...], preferred_element_type=F32
        )
        for f in range(frames):
            here = tokens[f * 128 : (f + 1) * 128] + feat + time_ref[f : f + 1, :]
            for part in range(3):
                tok_ref[part, pl.ds(f, 128, stride=frames), :] = here[
                    :, part * 128 : (part + 1) * 128
                ]
        fetch.wait()

    here = pl.ds(pl.multiple_of(step * CHUNK, CHUNK), CHUNK)
    tokens = jnp.concatenate([tok_ref[part, here, :] for part in range(3)], axis=1)
    normed = rms_scale(tokens, gain1_ref[...]).astype(BF16)
    keys = jnp.dot(normed, wk_ref[...], preferred_element_type=F32).astype(BF16)
    both = nt(wqv_ref[...], normed).astype(BF16)
    query, values = both[: HEADS * HEAD], both[HEADS * HEAD :]
    track = lax.broadcasted_iota(jnp.int32, (16, 128), 1) // frames
    frame = lax.broadcasted_iota(jnp.int32, (16, 128), 0)
    key_track = lax.broadcasted_iota(jnp.int32, (128, 128), 0) // frames
    query_track = lax.broadcasted_iota(jnp.int32, (128, 128), 1) // frames
    same = (key_track == query_track).astype(BF16)
    factor = HEAD ** -0.5 * 1.4426950408889634
    zeros16 = jnp.zeros((16, 128), BF16)
    zeros64 = jnp.zeros((64, 128), BF16)
    attended = []
    for first in range(0, CHUNK // 128, BATCH):
        some = range(first, first + BATCH)
        own, valid = [], []
        for g in some:
            lanes = slice(g * 128, (g + 1) * 128)
            valid += [frame >= start_ref[0, :, lanes]] * HEADS
            for pair in range(HEADS // 2):
                one = query[2 * pair * HEAD : (2 * pair + 1) * HEAD, lanes]
                two = query[(2 * pair + 1) * HEAD : (2 * pair + 2) * HEAD, lanes]
                both = jnp.concatenate(
                    [
                        jnp.concatenate([one, zeros16, zeros64], axis=0),
                        jnp.concatenate([zeros64, two, zeros16], axis=0),
                    ],
                    axis=1,
                )
                scores = jnp.dot(
                    keys[lanes, pair * 128 : (pair + 1) * 128], both, preferred_element_type=F32
                )
                for h in range(2):
                    full = scores[:, h * 128 : (h + 1) * 128]
                    part = full[0:16, :]
                    for t in range(1, 8):
                        part = jnp.where(track == t, full[16 * t : 16 * (t + 1), :], part)
                    own.append(part)
        own = [jnp.where(v, p, -1e30) for v, p in zip(valid, own)]
        top = [jnp.max(p, axis=0, keepdims=True) for p in own]
        weights = [jnp.exp2((p - t) * factor) for p, t in zip(own, top)]
        total = [jnp.sum(w, axis=0, keepdims=True) for w in weights]
        probs = [(w * (1.0 / t)).astype(BF16) for w, t in zip(weights, total)]
        for g in some:
            lanes = slice(g * 128, (g + 1) * 128)
            heads = []
            for pair in range(HEADS // 2):
                two = [
                    jnp.concatenate([probs[(g - first) * HEADS + 2 * pair + h]] * 8, axis=0) * same
                    for h in range(2)
                ]
                at = 2 * pair * HEAD
                both = jnp.dot(
                    values[at : at + 2 * HEAD, lanes],
                    jnp.concatenate(two, axis=1),
                    preferred_element_type=F32,
                )
                heads += [both[:HEAD, :128], both[HEAD:, 128:]]
            attended.append(jnp.concatenate(heads, axis=0).astype(BF16).T)
    attended = jnp.concatenate(attended, axis=0)
    mixed = tokens + jnp.dot(attended, wout_ref[...], preferred_element_type=F32)
    normed2 = rms_scale(mixed, gain2_ref[...]).astype(BF16)
    hidden = jax.nn.gelu(
        jnp.dot(normed2, wup_ref[...], preferred_element_type=F32), approximate=True
    ).astype(BF16)
    result = mixed + jnp.dot(hidden, down_ref[...], preferred_element_type=F32)
    out_ref[...] = result.astype(BF16)


def params(mib):
    return pltpu.CompilerParams(vmem_limit_bytes=mib << 20)


SMEM = pl.BlockSpec(memory_space=pltpu.SMEM)
VMEM = pl.BlockSpec(memory_space=pltpu.VMEM)
HBM = pl.BlockSpec(memory_space=pltpu.HBM)


def refine_call(height, raw, *rest):
    tokens, dim = rest[5].size, rest[4].shape[1]
    chans = raw.shape[1]
    step = pl.BlockSpec((1, 1, CHUNK), lambda i: (i, 0, 0))
    return pl.pallas_call(
        functools.partial(refine_kernel, height),
        grid=(tokens // CHUNK,),
        out_shape=jax.ShapeDtypeStruct((tokens, dim), BF16),
        in_specs=[VMEM] * 6 + [step] + [VMEM] * (len(rest) - 7) + [HBM],
        out_specs=pl.BlockSpec((CHUNK, dim), lambda i: (i, 0)),
        scratch_shapes=[
            pltpu.VMEM((raw.shape[0] + 32, 128), F32),
            pltpu.VMEM((tokens // 128 * 112, 9 * chans), BF16),
            pltpu.VMEM((3, tokens, 128), F32),
            pltpu.VMEM(rest[-1].shape, BF16),
            pltpu.SemaphoreType.DMA,
        ],
        compiler_params=params(32),
        name="refine",
    )(raw, *rest[:-1], pltpu.with_memory_space_constraint(rest[-1], pltpu.HBM))


def body(
    features, w_conv, query_feats, offset_rows, offset_cols, owners, start_frames, w_corr, w_feat,
    time_embed, gain_attn, w_qkv, w_attn_out, gain_mlp, w_up, w_down,
):
    n_tiles = lax.axis_size("tiles")
    frames, rows, width, chans = features.shape
    blocks = owners.shape[0]
    tracks = query_feats.shape[0]
    total = time_embed.shape[0]
    dim = w_feat.shape[1]

    owner = owners[:, 0]
    number = jnp.arange(blocks, dtype=jnp.int32)
    rank = jnp.sum(
        (owner[:, None] == owner[None, :]) & (number[None, :] < number[:, None]), axis=1, dtype=jnp.int32
    )
    hbm = lambda array: pltpu.with_memory_space_constraint(array, pltpu.HBM)
    pieces = pl.pallas_call(
        send_kernel,
        out_shape=pltpu.HBM((PIECES, SENT, chans), BF16),
        in_specs=[HBM] * 4,
        out_specs=HBM,
        scratch_shapes=[
            pltpu.SMEM((blocks,), jnp.int32),
            pltpu.SMEM(offset_cols.shape, jnp.int32),
            pltpu.SMEM(offset_rows.shape, jnp.int32),
            pltpu.VMEM(features.shape, BF16),
            pltpu.SMEM((64,), jnp.int32),
            pltpu.VMEM((TOGETHER, TILE, 48, 128), F32),
            pltpu.VMEM((TOGETHER, 192, 128), F32),
            pltpu.VMEM((PIECES * SENT, 128), F32),
            pltpu.VMEM((PIECES, SENT, chans), BF16),
            pltpu.SemaphoreType.DMA((3,)),
            pltpu.SemaphoreType.DMA((frames,)),
            pltpu.SemaphoreType.DMA((PIECES,)),
        ],
        compiler_params=params(32),
        name="windows",
    )(hbm(owner), hbm(offset_cols), hbm(offset_rows), hbm(features))
    spread = lax.all_to_all(
        pieces, "tiles", 0, 0, tiled=True, axis_index_groups=[list(range(n_tiles))[::-1]]
    )
    wk = jnp.pad(w_qkv[:, dim : 2 * dim].reshape(dim, HEADS, HEAD), ((0, 0), (0, 0), (0, 16)))
    wk = wk.reshape(dim, HEADS * 64)
    wqv = jnp.concatenate([w_qkv[:, :dim], w_qkv[:, 2 * dim :]], axis=1).T
    wcorr = jnp.pad(w_corr.reshape(WIN, WIN, dim), ((0, 0), (0, RAW - WIN), (0, 0)))
    wcorr = jnp.pad(wcorr.reshape(WIN * RAW, dim), ((0, 112 - WIN * RAW), (0, 0)))
    tokens = tracks * total
    start = jnp.repeat(start_frames, total).reshape(tokens // CHUNK, 1, CHUNK)
    gain1, gain2 = gain_attn.reshape(1, dim), gain_mlp.reshape(1, dim)
    first = (wk, wqv, hbm(wcorr), start, gain1, gain2)
    index = routes(owner, rank, offset_rows, n_tiles - 1 - lax.axis_index("tiles"), n_tiles, rows)
    routed = pl.pallas_call(
        route_kernel,
        out_shape=jax.ShapeDtypeStruct((blocks, PROWS, chans), BF16),
        in_specs=[HBM, VMEM] + [HBM] * len(first),
        out_specs=VMEM,
        scratch_shapes=[
            pltpu.SMEM(index.shape, jnp.int32),
            pltpu.VMEM((n_tiles * SENT + 16, 128), F32),
            pltpu.VMEM((blocks, 32, 128), F32),
            pltpu.SemaphoreType.DMA,
        ],
        compiler_params=params(32),
        name="route",
    )(index, spread, *first)
    raw = lax.all_to_all(routed, ("frames", "tiles"), 0, 0, tiled=True)
    raw = raw.reshape(blocks * PROWS, chans)

    refined = refine_call(
        n_tiles * rows, raw, w_conv.reshape(9 * chans, chans), query_feats, wcorr, w_feat, time_embed,
        start, gain1, wk, wqv, w_attn_out, gain2, w_up, w_down,
    )
    return refined.reshape(tracks, total, dim)


def solution(mesh):
    placed = (
        P("frames", "tiles", None, None),
        P(),
        P(("frames", "tiles"), None),
        P("frames", None),
        P("frames", None),
        P(),
        P(("frames", "tiles")),
        P(), P(), P(), P(), P(), P(), P(), P(), P(),
    )
    return jax.shard_map(
        body,
        mesh=mesh,
        in_specs=placed,
        out_specs=P(("frames", "tiles"), None, None),
        check_vma=False,
    )
```
